32 devices in a mesh: groups: 2 (over x), query: 8 (over z, y), target: 2 (over core).
Axes of the slice: x: 2, y: 2, z: 4, core: 2. Of those that a mesh axis runs over, the one named last changes fastest.
Arguments:
- query_input: bfloat16 [32, 960, 128], P(('groups', 'query')), parts along dimension 0, may hold values from -18 to 18
- target_input: bfloat16 [64, 960, 128], P(('groups', 'query', 'target')), parts along dimension 0, may hold values from -18 to 18
- conv_weight: bfloat16 [3, 3, 128, 128], replicated, may hold values from -0.1875 to 0.1875
- conv_bias: float32 [128], replicated, may hold values from -3 to 3
Outputs:
- flow: float32 [2, 16, 480], P(None, ('groups', 'query')), parts along dimension 1
The draws below stay inside these ranges and needn't reach their ends.
There are 2 independent parts, one for each index of `groups`. The reference program is written for one: setup_inputs(seed, part) draws one part's arguments, and reference() takes and returns one part's arrays. A program takes and returns all parts, laid end to end along the dimension named above; an argument that names none is the same for every part. Nothing has to cross between parts.
All inputs are finite; a program needn't handle non-finite values.
Results may differ from the reference program's by a relative error of at most 0.0026.
Values may be sent and summed in bfloat16 or wider, within the bound.
No kernel may reach another device: no remote copies, remote signals or barrier semaphores. Data moves between devices by JAX's collectives and lax.ppermute only.
A program may use at most 64 MiB of HBM per device.

```python
import math
import jax
import jax.numpy as jnp
from jax import lax

C = 128
CIN = 128
W = 480
QUERY_ROWS = 8
TARGET_ROWS = 16


def draw_frames(key):
    folded = jax.random.fold_in(key, 4111)
    key_query, key_target = jax.random.split(folded, 2)
    query_shape = (2 * QUERY_ROWS, 2 * W, CIN)
    target_shape = (2 * TARGET_ROWS, 2 * W, CIN)
    queries = jnp.clip(jax.random.normal(key_query, query_shape, jnp.float32), -6.0, 6.0)
    targets = jnp.clip(jax.random.normal(key_target, target_shape, jnp.float32), -6.0, 6.0)
    return (queries, targets)


def draw_query_input(key, part):
    return draw_frames(key)[0].astype(jnp.bfloat16)


def draw_target_input(key, part):
    return draw_frames(key)[1].astype(jnp.bfloat16)


def noise(own_key, shape, deviation, limit, held_as=jnp.bfloat16):
    values = deviation * jax.random.normal(own_key, shape, jnp.float32)
    return jnp.clip(values, min=-limit, max=limit).astype(held_as)


def setup_inputs(seed: int = 0, part: int = 0) -> dict:
    key_of = jax.random.split(jax.random.key(seed), 5)
    own_keys = jax.random.split(jax.random.fold_in(key_of[4], part), 5)
    query_input = draw_query_input(jax.random.fold_in(jax.random.fold_in(key_of[4], part), 71), part)
    target_input = draw_target_input(jax.random.fold_in(jax.random.fold_in(key_of[4], part), 71), part)
    conv_weight = noise(key_of[2], (3, 3, CIN, C), (9 * CIN) ** -0.5, 0.1875)
    conv_bias = noise(key_of[3], (C,), 0.5, 3.0, jnp.float32)
    return dict(query_input=query_input, target_input=target_input, conv_weight=conv_weight, conv_bias=conv_bias)


CELL = 0.0625

def convolve(frame, conv_weight, conv_bias):
    padded = jnp.pad(frame, ((1, 0), (1, 0), (0, 0)))
    out_rows = frame.shape[0] // 2
    out_cols = frame.shape[1] // 2
    channels = frame.shape[2]
    summed = jnp.zeros((out_rows * out_cols, conv_weight.shape[3]), jnp.float32)
    for tap_row in range(3):
        for tap_col in range(3):
            window = padded[tap_row:tap_row + 2 * out_rows:2, tap_col:tap_col + 2 * out_cols:2]
            summed = summed + jnp.dot(window.reshape(out_rows * out_cols, channels), conv_weight[tap_row, tap_col], preferred_element_type=jnp.float32)
    return (summed + conv_bias).astype(jnp.bfloat16)

def reference(query_input, target_input, conv_weight, conv_bias):
    queries = convolve(query_input, conv_weight, conv_bias)
    targets = convolve(target_input, conv_weight, conv_bias)
    positions = jnp.arange(TARGET_ROWS * W, dtype=jnp.int32)
    target_x = (positions % W).astype(jnp.float32) * CELL
    target_y = (positions // W).astype(jnp.float32) * CELL
    inv_root = 1.0 / math.sqrt(C)

    def match(band_queries):
        scores = jnp.dot(band_queries, targets.T, preferred_element_type=jnp.float32) * inv_root
        highest = lax.optimization_barrier(jnp.max(scores, axis=1, keepdims=True))
        weights = jnp.exp(scores - highest)
        weight_sum = lax.optimization_barrier(jnp.sum(weights, axis=1))
        sum_x = jnp.dot(weights, target_x, precision=lax.Precision.HIGHEST)
        sum_y = jnp.dot(weights, target_y, precision=lax.Precision.HIGHEST)
        return (sum_x / weight_sum, sum_y / weight_sum)
    mean_x, mean_y = lax.map(match, queries.reshape(QUERY_ROWS, W, C))
    query_x = jnp.arange(W, dtype=jnp.int32).astype(jnp.float32)[None, :] * CELL
    query_y = jnp.arange(QUERY_ROWS, dtype=jnp.int32).astype(jnp.float32)[:, None] * CELL
    return jnp.stack([mean_x - query_x, mean_y - query_y])
```

```python
import functools
import math

import jax
import jax.numpy as jnp
from jax import lax
from jax.experimental import pallas as pl
from jax.experimental.pallas import tpu as pltpu
from jax.sharding import PartitionSpec as P

CELL = 0.0625
LOG2E = math.log2(math.e)
VMEM_LIMIT = 32 * 1024 * 1024


def sent(value, axis, target_of):
    count = lax.axis_size(axis)
    route = [(i, target_of(i)) for i in range(count)]
    route = [(i, to) for i, to in route if 0 <= to < count]
    return lax.ppermute(value, axis, route)


def column_taps(row, stage):
    out_cols = row.shape[0] // 2
    stage[pl.ds(8, row.shape[0]), :] = row.astype(jnp.float32)
    return [
        stage[pl.ds(7 + tap, out_cols, stride=2), :].astype(jnp.bfloat16) for tap in range(3)
    ]


def tap_row_sum(row, weight_ref, tap_row, stage):
    taps = column_taps(row, stage)
    total = None
    for tap_col in range(3):
        term = jnp.dot(
            taps[tap_col], weight_ref[tap_row, tap_col], preferred_element_type=jnp.float32
        )
        total = term if total is None else total + term
    return total


def rim_kernel(query_ref, target_ref, weight_ref, query_rim_ref, target_rim_ref, *stages):
    for stage in stages:
        stage[pl.ds(0, 8), :] = jnp.zeros((8, stage.shape[1]), jnp.float32)
    pairs = ((query_ref, query_rim_ref), (target_ref, target_rim_ref))
    for (frame_ref, rim_ref), stage in zip(pairs, stages):
        rim_ref[...] = tap_row_sum(frame_ref[0], weight_ref, 0, stage).astype(rim_ref.dtype)


def rim_partials(query_input, target_input, conv_weight):
    rows, cols, channels = query_input.shape
    out_channels = conv_weight.shape[3]
    rim = jax.ShapeDtypeStruct((cols // 2, out_channels), jnp.bfloat16)
    last_row = pl.BlockSpec((1, cols, channels), lambda i: (rows - 1, 0, 0))
    first_taps = pl.BlockSpec((1,) + conv_weight.shape[1:], lambda i: (0, 0, 0, 0))
    whole = pl.BlockSpec((cols // 2, out_channels), lambda i: (0, 0))
    return pl.pallas_call(
        rim_kernel,
        grid=(1,),
        out_shape=(rim, rim),
        in_specs=[last_row, last_row, first_taps],
        out_specs=(whole, whole),
        scratch_shapes=[pltpu.VMEM((cols + 8, channels), jnp.float32)] * 2,
        compiler_params=pltpu.CompilerParams(vmem_limit_bytes=VMEM_LIMIT),
        name="rim_partials",
    )(query_input, target_input, conv_weight)


def own_kernel(query_ref, target_ref, weight_ref, bias_ref, query_out, target_out, *stages):
    for stage in stages:
        stage[pl.ds(0, 8), :] = jnp.zeros((8, stage.shape[1]), jnp.float32)
    for which, (frame_ref, out_ref) in enumerate(((query_ref, query_out), (target_ref, target_out))):
        total = bias_ref[...]
        for tap_row in (1, 2):
            total = total + tap_row_sum(
                frame_ref[tap_row - 1], weight_ref, tap_row, stages[2 * which + tap_row - 1]
            )
        out_ref[...] = total


def own_partials(query_input, target_input, conv_weight, conv_bias):
    rows, cols, channels = query_input.shape
    out_channels = conv_weight.shape[3]
    part = jax.ShapeDtypeStruct((cols // 2, out_channels), jnp.float32)
    flops = 2 * 2 * 6 * (cols // 2) * channels * out_channels
    return pl.pallas_call(
        own_kernel,
        out_shape=(part, part),
        scratch_shapes=[pltpu.VMEM((cols + 8, channels), jnp.float32)] * 4,
        compiler_params=pltpu.CompilerParams(vmem_limit_bytes=VMEM_LIMIT),
        cost_estimate=pl.CostEstimate(flops=flops, bytes_accessed=1 << 22, transcendentals=0),
        name="own_partials",
    )(query_input, target_input, conv_weight, conv_bias.reshape(1, out_channels))


def match_kernel(members, shares, row_y_ref, *refs):
    query_refs = refs[:members]
    target_refs = refs[members : members + shares]
    out_refs = refs[members + shares : 2 * members + shares]
    scores_refs = refs[2 * members + shares :]
    channels = query_refs[0].shape[1]
    row_width = target_refs[0].shape[0]
    lanes = query_refs[0].shape[0]
    steps = row_width // 8
    scale = LOG2E / math.sqrt(channels)
    for member in range(members):
        highest = None
        for share in range(shares):
            scores_ref = scores_refs[(member % 2) * shares + share]
            scores_ref[...] = lax.dot_general(
                target_refs[share][...],
                query_refs[member][...],
                (((1,), (1,)), ((), ())),
                preferred_element_type=jnp.float32,
            )
            for step in range(steps):
                block = scores_ref[pl.ds(8 * step, 8), :]
                highest = block if highest is None else jnp.maximum(highest, block)
        highest = jnp.max(highest, axis=0, keepdims=True)
        spread = jnp.broadcast_to(highest, (8, lanes))
        weight_sum = sum_x = sum_y = None
        offset = lax.broadcasted_iota(jnp.int32, (8, lanes), 0).astype(jnp.float32)
        for share in range(shares):
            scores_ref = scores_refs[(member % 2) * shares + share]
            plain = jnp.zeros((8, lanes), jnp.float32)
            stacked = jnp.zeros((8, lanes), jnp.float32)
            for step in reversed(range(steps)):
                weights = jnp.exp2((scores_ref[pl.ds(8 * step, 8), :] - spread) * scale)
                if step == 0:
                    plain = plain + weights
                else:
                    plain = plain + weights
                    stacked = stacked + plain
            part_x = jnp.sum(8.0 * stacked + offset * plain, axis=0, keepdims=True) * CELL
            part_sum = jnp.sum(plain, axis=0, keepdims=True)
            part_y = part_sum * row_y_ref[share]
            if weight_sum is None:
                weight_sum, sum_x, sum_y = part_sum, part_x, part_y
            else:
                weight_sum, sum_x, sum_y = weight_sum + part_sum, sum_x + part_x, sum_y + part_y
        out_refs[member][...] = jnp.concatenate([highest, weight_sum, sum_x, sum_y], axis=0)


def match(queries, targets, row_y):
    members, shares = len(queries), len(targets)
    lanes, channels = queries[0].shape
    row_width = targets[0].shape[0]
    vmem = pl.BlockSpec(memory_space=pltpu.VMEM)
    return pl.pallas_call(
        functools.partial(match_kernel, members, shares),
        out_shape=(jax.ShapeDtypeStruct((4, lanes), jnp.float32),) * members,
        in_specs=[pl.BlockSpec(memory_space=pltpu.SMEM)] + [vmem] * (members + shares),
        out_specs=(vmem,) * members,
        scratch_shapes=[pltpu.VMEM((row_width, lanes), jnp.float32)] * (2 * shares),
        compiler_params=pltpu.CompilerParams(vmem_limit_bytes=VMEM_LIMIT),
        cost_estimate=pl.CostEstimate(
            flops=2 * members * shares * lanes * row_width * channels,
            bytes_accessed=1 << 22,
            transcendentals=members * shares * lanes * row_width,
        ),
        name="match",
    )(row_y, *queries, *targets)


def combined(first, second, scale):
    highest = jnp.maximum(first[..., :1, :], second[..., :1, :])
    first_scale = jnp.exp2((first[..., :1, :] - highest) * scale)
    second_scale = jnp.exp2((second[..., :1, :] - highest) * scale)
    sums = first[..., 1:, :] * first_scale + second[..., 1:, :] * second_scale
    return jnp.concatenate([highest, sums], axis=-2)


def on_device(query_input, target_input, conv_weight, conv_bias):
    query_slot = lax.axis_index("query")
    core_slot = lax.axis_index("target")
    core_count = lax.axis_size("target")
    query_total = lax.axis_size("query")
    row_width = query_input.shape[1] // 2
    channels = conv_weight.shape[3]

    query_rim, target_rim = rim_partials(query_input, target_input, conv_weight)
    query_rim = sent(query_rim, "query", lambda i: i + 1)
    target_rim = sent(target_rim, ("query", "target"), lambda i: i + 1)
    query_part, target_part = own_partials(query_input, target_input, conv_weight, conv_bias)
    queries = (query_part + query_rim.astype(jnp.float32)).astype(jnp.bfloat16)
    targets = (target_part + target_rim.astype(jnp.float32)).astype(jnp.bfloat16)

    block_queries = [queries] + [
        sent(queries, "query", lambda i, member=member: i ^ member) for member in (1, 2, 3)
    ]
    shares = [targets]
    for _ in range(query_total // 4 - 1):
        shares.append(sent(shares[-1], "query", lambda i: (i + 4) % query_total))
    share_slots = [(query_slot - 4 * hop) % query_total for hop in range(query_total // 4)]
    row_y = jnp.stack(
        [(slot * core_count + core_slot).astype(jnp.float32) * CELL for slot in share_slots]
    )
    states = match(block_queries, shares, row_y)

    scale = LOG2E / math.sqrt(channels)
    near = sent(jnp.concatenate([states[1], states[3]], axis=0), "query", lambda i: i ^ 1)
    own = combined(states[0], near[:4], scale)
    other = combined(states[2], near[4:], scale)
    own = combined(own, sent(other, "query", lambda i: i ^ 2), scale)
    total = combined(own, sent(own, "target", lambda i: i ^ 1), scale)
    columns = jnp.arange(row_width, dtype=jnp.int32).astype(jnp.float32) * CELL
    flow_x = total[2] / total[1] - columns
    flow_y = total[3] / total[1] - query_slot.astype(jnp.float32) * CELL
    return jnp.stack([flow_x, flow_y]).reshape(2, 1, row_width)


def solution(mesh):
    placed = (
        P(("groups", "query"), None, None),
        P(("groups", "query", "target"), None, None),
        P(),
        P(),
    )
    return jax.shard_map(
        on_device,
        mesh=mesh,
        in_specs=placed,
        out_specs=P(None, ("groups", "query"), None),
        check_vma=False,
    )
```

```python
import functools
import math

import jax
import jax.numpy as jnp
from jax import lax
from jax.experimental import pallas as pl
from jax.experimental.pallas import tpu as pltpu
from jax.sharding import PartitionSpec as P

CELL = 0.0625
LOG2E = math.log2(math.e)
VMEM_LIMIT = 32 * 1024 * 1024


def sent(value, axis, target_of):
    count = lax.axis_size(axis)
    route = [(i, target_of(i)) for i in range(count)]
    route = [(i, to) for i, to in route if 0 <= to < count]
    return lax.ppermute(value, axis, route)


def column_taps(row, stage):
    out_cols = row.shape[0] // 2
    stage[pl.ds(8, row.shape[0]), :] = row.astype(jnp.float32)
    return [
        stage[pl.ds(7 + tap, out_cols, stride=2), :].astype(jnp.bfloat16) for tap in range(3)
    ]


def tap_row_sum(row, weight_ref, tap_row, stage):
    taps = column_taps(row, stage)
    total = None
    for tap_col in range(3):
        term = jnp.dot(
            taps[tap_col], weight_ref[tap_row, tap_col], preferred_element_type=jnp.float32
        )
        total = term if total is None else total + term
    return total


def rim_kernel(query_hbm, target_hbm, weight_hbm, rim_ref, rows_ref, taps_ref, sems, *stages):
    last = query_hbm.shape[0] - 1
    out_cols = rim_ref.shape[0] // 2
    copies = [
        pltpu.make_async_copy(weight_hbm.at[pl.ds(0, 1)], taps_ref, sems.at[2]),
        pltpu.make_async_copy(target_hbm.at[last], rows_ref.at[0], sems.at[0]),
        pltpu.make_async_copy(query_hbm.at[last], rows_ref.at[1], sems.at[1]),
    ]
    for copy in copies:
        copy.start()
    for stage in stages:
        stage[pl.ds(0, 8), :] = jnp.zeros((8, stage.shape[1]), jnp.float32)
    for copy in copies:
        copy.wait()
    for which, stage in enumerate(stages):
        rim_ref[pl.ds(which * out_cols, out_cols), :] = tap_row_sum(
            rows_ref[which], taps_ref, 0, stage
        ).astype(rim_ref.dtype)


def rim_partials(query_input, target_input, conv_weight):
    _, cols, channels = query_input.shape
    out_channels = conv_weight.shape[3]
    hbm = pl.BlockSpec(memory_space=pltpu.HBM)
    return pl.pallas_call(
        rim_kernel,
        out_shape=jax.ShapeDtypeStruct((cols, out_channels), jnp.bfloat16),
        in_specs=[hbm] * 3,
        out_specs=pl.BlockSpec(memory_space=pltpu.VMEM),
        scratch_shapes=[
            pltpu.VMEM((2, cols, channels), jnp.bfloat16),
            pltpu.VMEM((1,) + conv_weight.shape[1:], jnp.bfloat16),
            pltpu.SemaphoreType.DMA((3,)),
        ]
        + [pltpu.VMEM((cols + 8, channels), jnp.float32)] * 2,
        compiler_params=pltpu.CompilerParams(vmem_limit_bytes=VMEM_LIMIT),
        name="rim_partials",
    )(query_input, target_input, conv_weight)


def own_kernel(
    query_hbm, target_hbm, weight_hbm, bias_ref, query_out, target_out, frames, taps_ref, sems, *stages
):
    copies = [
        pltpu.make_async_copy(query_hbm, frames.at[0], sems.at[0]),
        pltpu.make_async_copy(target_hbm, frames.at[1], sems.at[1]),
        pltpu.make_async_copy(weight_hbm, taps_ref, sems.at[2]),
    ]
    for copy in copies:
        copy.start()
    for stage in stages:
        stage[pl.ds(0, 8), :] = jnp.zeros((8, stage.shape[1]), jnp.float32)
    for copy in copies:
        copy.wait()
    for which, out_ref in enumerate((query_out, target_out)):
        total = bias_ref[...]
        for tap_row in (1, 2):
            total = total + tap_row_sum(
                frames[which, tap_row - 1], taps_ref, tap_row, stages[2 * which + tap_row - 1]
            )
        out_ref[...] = total


def own_partials(query_input, target_input, conv_weight, conv_bias):
    rows, cols, channels = query_input.shape
    out_channels = conv_weight.shape[3]
    part = jax.ShapeDtypeStruct((cols // 2, out_channels), jnp.float32)
    flops = 2 * 2 * 6 * (cols // 2) * channels * out_channels
    return pl.pallas_call(
        own_kernel,
        out_shape=(part, part),
        in_specs=[pl.BlockSpec(memory_space=pltpu.HBM)] * 3 + [pl.BlockSpec(memory_space=pltpu.VMEM)],
        out_specs=(pl.BlockSpec(memory_space=pltpu.VMEM),) * 2,
        scratch_shapes=[
            pltpu.VMEM((2, rows, cols, channels), jnp.bfloat16),
            pltpu.VMEM(conv_weight.shape, jnp.bfloat16),
            pltpu.SemaphoreType.DMA((3,)),
        ]
        + [pltpu.VMEM((cols + 8, channels), jnp.float32)] * 4,
        compiler_params=pltpu.CompilerParams(vmem_limit_bytes=VMEM_LIMIT),
        cost_estimate=pl.CostEstimate(flops=flops, bytes_accessed=1 << 22, transcendentals=0),
        name="own_partials",
    )(query_input, target_input, conv_weight, conv_bias.reshape(1, out_channels))


def match_kernel(members, shares, row_y_ref, *refs):
    query_refs = refs[:members]
    target_refs = refs[members : members + shares]
    out_refs = refs[members + shares : 2 * members + shares]
    scores_refs = refs[2 * members + shares :]
    channels = query_refs[0].shape[1]
    row_width = target_refs[0].shape[0]
    lanes = query_refs[0].shape[0]
    steps = row_width // 8
    scale = LOG2E / math.sqrt(channels)
    for member in range(members):
        highest = None
        for share in range(shares):
            scores_ref = scores_refs[(member % 2) * shares + share]
            scores_ref[...] = lax.dot_general(
                target_refs[share][...],
                query_refs[member][...],
                (((1,), (1,)), ((), ())),
                preferred_element_type=jnp.float32,
            )
            for step in range(steps):
                block = scores_ref[pl.ds(8 * step, 8), :]
                highest = block if highest is None else jnp.maximum(highest, block)
        highest = jnp.max(highest, axis=0, keepdims=True)
        spread = jnp.broadcast_to(highest, (8, lanes))
        weight_sum = sum_x = sum_y = None
        offset = lax.broadcasted_iota(jnp.int32, (8, lanes), 0).astype(jnp.float32)
        for share in range(shares):
            scores_ref = scores_refs[(member % 2) * shares + share]
            plain = jnp.zeros((8, lanes), jnp.float32)
            stacked = jnp.zeros((8, lanes), jnp.float32)
            for step in reversed(range(steps)):
                weights = jnp.exp2((scores_ref[pl.ds(8 * step, 8), :] - spread) * scale)
                if step == 0:
                    plain = plain + weights
                else:
                    plain = plain + weights
                    stacked = stacked + plain
            part_x = jnp.sum(8.0 * stacked + offset * plain, axis=0, keepdims=True) * CELL
            part_sum = jnp.sum(plain, axis=0, keepdims=True)
            part_y = part_sum * row_y_ref[share]
            if weight_sum is None:
                weight_sum, sum_x, sum_y = part_sum, part_x, part_y
            else:
                weight_sum, sum_x, sum_y = weight_sum + part_sum, sum_x + part_x, sum_y + part_y
        out_refs[member][...] = jnp.concatenate([highest, weight_sum, sum_x, sum_y], axis=0)


def match(queries, targets, row_y):
    members, shares = len(queries), len(targets)
    lanes, channels = queries[0].shape
    row_width = targets[0].shape[0]
    vmem = pl.BlockSpec(memory_space=pltpu.VMEM)
    return pl.pallas_call(
        functools.partial(match_kernel, members, shares),
        out_shape=(jax.ShapeDtypeStruct((4, lanes), jnp.float32),) * members,
        in_specs=[pl.BlockSpec(memory_space=pltpu.SMEM)] + [vmem] * (members + shares),
        out_specs=(vmem,) * members,
        scratch_shapes=[pltpu.VMEM((row_width, lanes), jnp.float32)] * (2 * shares),
        compiler_params=pltpu.CompilerParams(vmem_limit_bytes=VMEM_LIMIT),
        cost_estimate=pl.CostEstimate(
            flops=2 * members * shares * lanes * row_width * channels,
            bytes_accessed=1 << 22,
            transcendentals=members * shares * lanes * row_width,
        ),
        name="match",
    )(row_y, *queries, *targets)


def combined(first, second, scale):
    highest = jnp.maximum(first[..., :1, :], second[..., :1, :])
    first_scale = jnp.exp2((first[..., :1, :] - highest) * scale)
    second_scale = jnp.exp2((second[..., :1, :] - highest) * scale)
    sums = first[..., 1:, :] * first_scale + second[..., 1:, :] * second_scale
    return jnp.concatenate([highest, sums], axis=-2)


def routed(value, route):
    slots, cores = lax.axis_size("query"), lax.axis_size("target")
    pairs = []
    for slot in range(slots):
        for core in range(cores):
            to = route(slot, core)
            if to is not None:
                pairs.append((slot * cores + core, to[0] * cores + to[1]))
    return lax.ppermute(value, ("query", "target"), pairs)


def on_device(query_input, target_input, conv_weight, conv_bias):
    slot = lax.axis_index("query")
    core = lax.axis_index("target")
    slots, cores = lax.axis_size("query"), lax.axis_size("target")
    row_width = query_input.shape[1] // 2
    channels = conv_weight.shape[3]
    scale = LOG2E / math.sqrt(channels)
    group = slots // 4
    first_core = core == 0

    def line(s, member):
        return (s // group ^ member) * group + s % group

    def near(s, hop):
        return s // group * group + (s + hop) % group

    rim = rim_partials(query_input, target_input, conv_weight)
    rim = routed(rim, lambda s, c: (s, 1) if c == 0 else ((s + 1) % slots, 0))
    rim = jnp.where((slot == 0) & first_core, 0, rim.astype(jnp.float32))
    query_part, target_part = own_partials(query_input, target_input, conv_weight, conv_bias)
    queries = (query_part + rim[row_width:]).astype(jnp.bfloat16)
    targets = (target_part + rim[:row_width]).astype(jnp.bfloat16)

    rows = [targets, routed(targets, lambda s, c: (s, 1 - c))]
    row_ids = [slot * cores + core, slot * cores + 1 - core]
    for hop in range(1, group):
        rows.append(routed(targets, lambda s, c: (near(s, hop), c)))
        row_ids.append(near(slot, -hop) * cores + core)
    far = routed(queries, lambda s, c: (line(s, 3), 1) if c == 0 else (s, 0))
    mid = routed(queries, lambda s, c: (line(s, 2), 1) if c == 0 else (s, 0))
    close = routed(queries, lambda s, c: (line(s, 1), 0) if c == 0 else (near(s, 1), 1))
    for hop in range(1, group):
        rows.append(routed(rows[hop + 1], lambda s, c: (s, 1 - c)))
        row_ids.append(near(slot, -hop) * cores + 1 - core)
    row_y = jnp.stack(row_ids).astype(jnp.float32) * CELL

    (late,) = match([jnp.where(first_core, queries, far)], rows, row_y)
    (early,) = match([jnp.where(first_core, close, mid)], rows, row_y)
    far_part = routed(late, lambda s, c: (line(s, 3), c))
    part = routed(early, lambda s, c: (line(s, 1 + c), c))
    own = combined(jnp.where(first_core, late, far_part), part, scale)
    total = combined(own, routed(own, lambda s, c: (s, 1 - c)), scale)
    columns = jnp.arange(row_width, dtype=jnp.int32).astype(jnp.float32) * CELL
    flow_x = total[2] / total[1] - columns
    flow_y = total[3] / total[1] - slot.astype(jnp.float32) * CELL
    return jnp.stack([flow_x, flow_y]).reshape(2, 1, row_width)


def solution(mesh):
    placed = (
        P(("groups", "query"), None, None),
        P(("groups", "query", "target"), None, None),
        P(),
        P(),
    )
    return jax.shard_map(
        on_device,
        mesh=mesh,
        in_specs=placed,
        out_specs=P(None, ("groups", "query"), None),
        check_vma=False,
    )
```

```python
import functools
import math

import jax
import jax.numpy as jnp
from jax import lax
from jax.experimental import pallas as pl
from jax.experimental.pallas import tpu as pltpu
from jax.sharding import PartitionSpec as P

CELL = 0.0625
LOG2E = math.log2(math.e)
VMEM_LIMIT = 32 * 1024 * 1024
RIM_VMEM = (64 * 1024 - 10752) * 1024


def column_taps(row, stage):
    out_cols = row.shape[0] // 2
    stage[pl.ds(8, row.shape[0]), :] = row.astype(jnp.float32)
    return [
        stage[pl.ds(7 + tap, out_cols, stride=2), :].astype(jnp.bfloat16) for tap in range(3)
    ]


def tap_row_sum(row, weight_ref, tap_row, stage):
    taps = column_taps(row, stage)
    total = None
    for tap_col in range(3):
        term = jnp.dot(
            taps[tap_col], weight_ref[tap_row, tap_col], preferred_element_type=jnp.float32
        )
        total = term if total is None else total + term
    return total


def rim_kernel(
    first_core_ref, query_hbm, target_hbm, weight_hbm, far_rim_ref, near_rim_ref, rows_ref, taps_ref, sems, *stages
):
    last = query_hbm.shape[0] - 1
    copies = [
        pltpu.make_async_copy(weight_hbm.at[pl.ds(0, 1)], taps_ref, sems.at[2]),
        pltpu.make_async_copy(target_hbm.at[last], rows_ref.at[0], sems.at[0]),
        pltpu.make_async_copy(query_hbm.at[last], rows_ref.at[1], sems.at[1]),
    ]
    for copy in copies:
        copy.start()
    for stage in stages:
        stage[pl.ds(0, 8), :] = jnp.zeros((8, stage.shape[1]), jnp.float32)
    for copy in copies:
        copy.wait()
    target_rim = tap_row_sum(rows_ref[0], taps_ref, 0, stages[0])
    query_rim = tap_row_sum(rows_ref[1], taps_ref, 0, stages[1])
    near_rim_ref[...] = target_rim.astype(near_rim_ref.dtype)
    far_rim_ref[...] = jnp.where(first_core_ref[0] == 1, query_rim, target_rim).astype(far_rim_ref.dtype)


def rim_partials(first_core, query_input, target_input, conv_weight):
    _, cols, channels = query_input.shape
    out_channels = conv_weight.shape[3]
    hbm = pl.BlockSpec(memory_space=pltpu.HBM)
    return pl.pallas_call(
        rim_kernel,
        out_shape=(jax.ShapeDtypeStruct((cols // 2, out_channels), jnp.bfloat16),) * 2,
        in_specs=[pl.BlockSpec(memory_space=pltpu.SMEM)] + [hbm] * 3,
        out_specs=(pl.BlockSpec(memory_space=pltpu.VMEM),) * 2,
        scratch_shapes=[
            pltpu.VMEM((2, cols, channels), jnp.bfloat16),
            pltpu.VMEM((1,) + conv_weight.shape[1:], jnp.bfloat16),
            pltpu.SemaphoreType.DMA((3,)),
        ]
        + [pltpu.VMEM((cols + 8, channels), jnp.float32)] * 2,
        compiler_params=pltpu.CompilerParams(vmem_limit_bytes=RIM_VMEM),
        name="rim_partials",
    )(first_core, query_input, target_input, conv_weight)


def own_kernel(query_ref, target_ref, weight_ref, bias_ref, query_out, target_out, *stages):
    for stage in stages:
        stage[pl.ds(0, 8), :] = jnp.zeros((8, stage.shape[1]), jnp.float32)
    pairs = ((target_ref, target_out), (query_ref, query_out))
    for which, (frame_ref, out_ref) in enumerate(pairs):
        total = bias_ref[...]
        for tap_row in (1, 2):
            total = total + tap_row_sum(
                frame_ref[tap_row - 1], weight_ref, tap_row, stages[2 * which + tap_row - 1]
            )
        out_ref[...] = total


def own_partials(query_input, target_input, conv_weight, conv_bias):
    _, cols, channels = query_input.shape
    out_channels = conv_weight.shape[3]
    part = jax.ShapeDtypeStruct((cols // 2, out_channels), jnp.float32)
    flops = 2 * 2 * 6 * (cols // 2) * channels * out_channels
    return pl.pallas_call(
        own_kernel,
        out_shape=(part, part),
        scratch_shapes=[pltpu.VMEM((cols + 8, channels), jnp.float32)] * 4,
        compiler_params=pltpu.CompilerParams(vmem_limit_bytes=VMEM_LIMIT),
        cost_estimate=pl.CostEstimate(flops=flops, bytes_accessed=1 << 22, transcendentals=0),
        name="own_partials",
    )(query_input, target_input, conv_weight, conv_bias.reshape(1, out_channels))


def merged(state, part, scale):
    top = jnp.maximum(state[0], part[0])
    keep = jnp.exp2((state[0] - top) * scale)
    gain = jnp.exp2((part[0] - top) * scale)
    return (top, *[old * keep + new * gain for old, new in zip(state[1:], part[1:])])


def match_kernel(shares, row_y_ref, query_ref, *refs):
    target_refs = refs[:shares]
    state_refs = refs[shares : -1 - shares]
    out_ref = refs[-1 - shares]
    scores_refs = refs[-shares:]
    lanes, channels = query_ref.shape
    steps = target_refs[0].shape[0] // 8
    scale = LOG2E / math.sqrt(channels)
    offset = lax.broadcasted_iota(jnp.int32, (8, lanes), 0).astype(jnp.float32)
    state = None
    for state_ref in state_refs:
        state = tuple(state_ref[pl.ds(i, 1), :] for i in range(4))
    for share in range(shares):
        scores_ref = scores_refs[share]
        scores_ref[...] = lax.dot_general(
            target_refs[share][...],
            query_ref[...],
            (((1,), (1,)), ((), ())),
            preferred_element_type=jnp.float32,
        )
        highest = scores_ref[pl.ds(0, 8), :]
        for step in range(1, steps):
            highest = jnp.maximum(highest, scores_ref[pl.ds(8 * step, 8), :])
        highest = jnp.max(highest, axis=0, keepdims=True)
        spread = jnp.broadcast_to(highest, (8, lanes))
        plain = jnp.zeros((8, lanes), jnp.float32)
        stacked = jnp.zeros((8, lanes), jnp.float32)
        for step in reversed(range(steps)):
            plain = plain + jnp.exp2((scores_ref[pl.ds(8 * step, 8), :] - spread) * scale)
            if step:
                stacked = stacked + plain
        part_x = jnp.sum(8.0 * stacked + offset * plain, axis=0, keepdims=True) * CELL
        part_sum = jnp.sum(plain, axis=0, keepdims=True)
        part = (highest, part_sum, part_x, part_sum * row_y_ref[share])
        state = part if state is None else merged(state, part, scale)
    out_ref[...] = jnp.concatenate(state, axis=0)


def match(queries, targets, row_y, state=None):
    shares = len(targets)
    lanes, channels = queries.shape
    row_width = targets[0].shape[0]
    states = [] if state is None else [state]
    vmem = pl.BlockSpec(memory_space=pltpu.VMEM)
    return pl.pallas_call(
        functools.partial(match_kernel, shares),
        out_shape=jax.ShapeDtypeStruct((4, lanes), jnp.float32),
        in_specs=[pl.BlockSpec(memory_space=pltpu.SMEM)] + [vmem] * (1 + shares + len(states)),
        out_specs=vmem,
        scratch_shapes=[pltpu.VMEM((row_width, lanes), jnp.float32)] * shares,
        compiler_params=pltpu.CompilerParams(vmem_limit_bytes=VMEM_LIMIT),
        cost_estimate=pl.CostEstimate(
            flops=2 * shares * lanes * row_width * channels,
            bytes_accessed=1 << 22,
            transcendentals=shares * lanes * row_width,
        ),
        name="match",
    )(row_y, queries, *targets, *states)


def combined(first, second, scale):
    highest = jnp.maximum(first[..., :1, :], second[..., :1, :])
    first_scale = jnp.exp2((first[..., :1, :] - highest) * scale)
    second_scale = jnp.exp2((second[..., :1, :] - highest) * scale)
    sums = first[..., 1:, :] * first_scale + second[..., 1:, :] * second_scale
    return jnp.concatenate([highest, sums], axis=-2)


def routed(value, route):
    slots, cores = lax.axis_size("query"), lax.axis_size("target")
    pairs = []
    for slot in range(slots):
        for core in range(cores):
            to = route(slot, core)
            if to is not None:
                pairs.append((slot * cores + core, to[0] * cores + to[1]))
    return lax.ppermute(value, ("query", "target"), pairs)


def on_device(query_input, target_input, conv_weight, conv_bias):
    slot = lax.axis_index("query")
    core = lax.axis_index("target")
    slots = lax.axis_size("query")
    row_width = query_input.shape[1] // 2
    channels = conv_weight.shape[3]
    scale = LOG2E / math.sqrt(channels)
    first = core == 0

    def pick(on_first, on_second):
        return jnp.where(first, on_first, on_second)

    def swapped(value):
        return routed(value, lambda s, c: (s, 1 - c))

    far_rim, near_rim = rim_partials(
        first.astype(jnp.int32).reshape(1), query_input, target_input, conv_weight
    )
    near_rim = swapped(near_rim)
    far_rim = routed(far_rim, lambda s, c: ((s + 1) % slots, c)).astype(jnp.float32)
    far_rim = jnp.where(slot == 0, 0.0, far_rim)
    query_part, target_part = own_partials(query_input, target_input, conv_weight, conv_bias)
    odd = (target_part + pick(0.0, near_rim.astype(jnp.float32))).astype(jnp.bfloat16)
    handed = swapped(odd)
    odd_away = [
        routed(odd, lambda s, c: (s, 1) if c == 0 else ((s + 4 * hop) % slots, 0))
        for hop in range(1, max(2, slots // 4))
    ]
    whole = (pick(query_part, handed.astype(jnp.float32)) + far_rim).astype(jnp.bfloat16)
    even_away = [
        routed(whole, lambda s, c: (s ^ 2, 0) if c == 0 else ((s + 4 * hop) % slots, 1))
        for hop in range(1, max(2, slots // 4))
    ]
    corner = routed(whole, lambda s, c: (s ^ 3, 1) if c == 0 else (s, 0))
    beside = routed(whole, lambda s, c: (s ^ 1, 1) if c == 0 else (s, 0))

    def row_y(ids):
        return jnp.stack(ids).astype(jnp.float32) * CELL

    members = [pick(whole, corner), pick(even_away[0], beside)]
    rows = [pick(corner, whole), pick(handed, odd)]
    ids = row_y([2 * slot, 2 * slot + 1])
    states = [match(member, rows, ids) for member in members]
    for hop in range(1, slots // 4):
        source = (slot - 4 * hop) % slots
        row = pick(odd_away[hop - 1], even_away[hop - 1])
        rows = [row, swapped(row)]
        ids = row_y([2 * source + 1 - core, 2 * source + core])
        states = [match(member, rows, ids, state) for member, state in zip(members, states)]
    state, other = states
    corner_state = routed(state, lambda s, c: (s ^ 3, c))
    other = routed(other, lambda s, c: (s ^ (2 if c == 0 else 1), c))
    own = combined(pick(state, corner_state), other, scale)
    total = combined(own, swapped(own), scale)
    columns = jnp.arange(row_width, dtype=jnp.int32).astype(jnp.float32) * CELL
    flow_x = total[2] / total[1] - columns
    flow_y = total[3] / total[1] - slot.astype(jnp.float32) * CELL
    return jnp.stack([flow_x, flow_y]).reshape(2, 1, row_width)


def solution(mesh):
    placed = (
        P(("groups", "query"), None, None),
        P(("groups", "query", "target"), None, None),
        P(),
        P(),
    )
    return jax.shard_map(
        on_device,
        mesh=mesh,
        in_specs=placed,
        out_specs=P(None, ("groups", "query"), None),
        check_vma=False,
    )
```

```python
import functools
import math

import jax
import jax.numpy as jnp
from jax import lax
from jax.experimental import pallas as pl
from jax.experimental.pallas import tpu as pltpu
from jax.sharding import PartitionSpec as P

CELL = 0.0625
LOG2E = math.log2(math.e)
VMEM_LIMIT = 32 * 1024 * 1024
RIM_VMEM = (64 * 1024 - 10752) * 1024


def column_taps(row, stage):
    out_cols = row.shape[0] // 2
    stage[pl.ds(8, row.shape[0]), :] = row.astype(jnp.float32)
    return [
        stage[pl.ds(7 + tap, out_cols, stride=2), :].astype(jnp.bfloat16) for tap in range(3)
    ]


def tap_row_sum(row, weight_ref, tap_row, stage):
    taps = column_taps(row, stage)
    total = None
    for tap_col in range(3):
        term = jnp.dot(
            taps[tap_col], weight_ref[tap_row, tap_col], preferred_element_type=jnp.float32
        )
        total = term if total is None else total + term
    return total


def rim_kernel(
    query_hbm, target_hbm, weight_hbm, far_rim_ref, near_rim_ref, rows_ref, taps_ref, sems, *stages
):
    first = lax.axis_index("target") == 0
    last = query_hbm.shape[0] - 1
    copies = [
        pltpu.make_async_copy(weight_hbm.at[pl.ds(0, 1)], taps_ref, sems.at[2]),
        pltpu.make_async_copy(target_hbm.at[last], rows_ref.at[0], sems.at[0]),
        pltpu.make_async_copy(query_hbm.at[last], rows_ref.at[1], sems.at[1]),
    ]
    for copy in copies:
        copy.start()
    for stage in stages:
        stage[pl.ds(0, 8), :] = jnp.zeros((8, stage.shape[1]), jnp.float32)
    for copy in copies:
        copy.wait()
    target_rim = tap_row_sum(rows_ref[0], taps_ref, 0, stages[0])
    query_rim = tap_row_sum(rows_ref[1], taps_ref, 0, stages[1])
    near_rim_ref[...] = target_rim.astype(near_rim_ref.dtype)
    far_rim_ref[...] = jnp.where(first, query_rim, target_rim).astype(far_rim_ref.dtype)


def rim_partials(query_input, target_input, conv_weight):
    _, cols, channels = query_input.shape
    out_channels = conv_weight.shape[3]
    hbm = pl.BlockSpec(memory_space=pltpu.HBM)
    return pl.pallas_call(
        rim_kernel,
        out_shape=(jax.ShapeDtypeStruct((cols // 2, out_channels), jnp.bfloat16),) * 2,
        in_specs=[hbm] * 3,
        out_specs=(pl.BlockSpec(memory_space=pltpu.VMEM),) * 2,
        scratch_shapes=[
            pltpu.VMEM((2, cols, channels), jnp.bfloat16),
            pltpu.VMEM((1,) + conv_weight.shape[1:], jnp.bfloat16),
            pltpu.SemaphoreType.DMA((3,)),
        ]
        + [pltpu.VMEM((cols + 8, channels), jnp.float32)] * 2,
        compiler_params=pltpu.CompilerParams(vmem_limit_bytes=RIM_VMEM),
        name="rim_partials",
    )(query_input, target_input, conv_weight)


def own_kernel(query_ref, target_ref, weight_ref, bias_ref, query_out, target_out, *stages):
    for stage in stages:
        stage[pl.ds(0, 8), :] = jnp.zeros((8, stage.shape[1]), jnp.float32)
    pairs = ((target_ref, target_out), (query_ref, query_out))
    for which, (frame_ref, out_ref) in enumerate(pairs):
        total = bias_ref[...]
        for tap_row in (1, 2):
            total = total + tap_row_sum(
                frame_ref[tap_row - 1], weight_ref, tap_row, stages[2 * which + tap_row - 1]
            )
        out_ref[...] = total


def own_partials(query_input, target_input, conv_weight, conv_bias):
    _, cols, channels = query_input.shape
    out_channels = conv_weight.shape[3]
    part = jax.ShapeDtypeStruct((cols // 2, out_channels), jnp.float32)
    flops = 2 * 2 * 6 * (cols // 2) * channels * out_channels
    return pl.pallas_call(
        own_kernel,
        out_shape=(part, part),
        scratch_shapes=[pltpu.VMEM((cols + 8, channels), jnp.float32)] * 4,
        compiler_params=pltpu.CompilerParams(vmem_limit_bytes=VMEM_LIMIT),
        cost_estimate=pl.CostEstimate(flops=flops, bytes_accessed=1 << 22, transcendentals=0),
        name="own_partials",
    )(query_input, target_input, conv_weight, conv_bias.reshape(1, out_channels))


def merged(state, part, scale):
    top = jnp.maximum(state[0], part[0])
    keep = jnp.exp2((state[0] - top) * scale)
    gain = jnp.exp2((part[0] - top) * scale)
    return (top, *[old * keep + new * gain for old, new in zip(state[1:], part[1:])])


def match_kernel(row_ids, *refs):
    core = lax.axis_index("target")
    query_refs, target_refs = refs[:2], refs[2:6]
    state_refs, out_ref, scores_refs = refs[6:-3], refs[-3], refs[-2:]
    lanes, channels = query_refs[0].shape
    steps = target_refs[0].shape[0] // 8
    scale = LOG2E / math.sqrt(channels)
    queries = jnp.where(core == 0, query_refs[0][...], query_refs[1][...])
    offset = lax.broadcasted_iota(jnp.int32, (8, lanes), 0).astype(jnp.float32)
    for share, scores_ref in enumerate(scores_refs):
        first_ref, second_ref = target_refs[2 * share : 2 * share + 2]
        targets = jnp.where(core == 0, first_ref[...], second_ref[...])
        scores_ref[...] = lax.dot_general(
            targets, queries, (((1,), (1,)), ((), ())), preferred_element_type=jnp.float32
        )
    state = None
    for state_ref in state_refs:
        state = tuple(state_ref[pl.ds(i, 1), :] for i in range(4))
    for row_id, scores_ref in zip(row_ids(lax.axis_index("query"), core), scores_refs):
        highest = scores_ref[pl.ds(0, 8), :]
        for step in range(1, steps):
            highest = jnp.maximum(highest, scores_ref[pl.ds(8 * step, 8), :])
        highest = jnp.max(highest, axis=0, keepdims=True)
        spread = jnp.broadcast_to(highest, (8, lanes))
        plain = jnp.zeros((8, lanes), jnp.float32)
        stacked = jnp.zeros((8, lanes), jnp.float32)
        for step in reversed(range(steps)):
            plain = plain + jnp.exp2((scores_ref[pl.ds(8 * step, 8), :] - spread) * scale)
            if step:
                stacked = stacked + plain
        part_x = jnp.sum(8.0 * stacked + offset * plain, axis=0, keepdims=True) * CELL
        part_sum = jnp.sum(plain, axis=0, keepdims=True)
        part = (highest, part_sum, part_x, part_sum * (row_id.astype(jnp.float32) * CELL))
        state = part if state is None else merged(state, part, scale)
    out_ref[...] = jnp.concatenate(state, axis=0)


def match(queries, targets, row_ids, state=None):
    lanes, channels = queries[0].shape
    row_width = targets[0][0].shape[0]
    operands = [*queries, *targets[0], *targets[1]] + ([] if state is None else [state])
    vmem = pl.BlockSpec(memory_space=pltpu.VMEM)
    return pl.pallas_call(
        functools.partial(match_kernel, row_ids),
        out_shape=jax.ShapeDtypeStruct((4, lanes), jnp.float32),
        in_specs=[vmem] * len(operands),
        out_specs=vmem,
        scratch_shapes=[pltpu.VMEM((row_width, lanes), jnp.float32)] * 2,
        compiler_params=pltpu.CompilerParams(vmem_limit_bytes=VMEM_LIMIT),
        cost_estimate=pl.CostEstimate(
            flops=4 * lanes * row_width * channels,
            bytes_accessed=1 << 22,
            transcendentals=2 * lanes * row_width,
        ),
        name="match",
    )(*operands)


def combined(first, second, scale):
    highest = jnp.maximum(first[..., :1, :], second[..., :1, :])
    first_scale = jnp.exp2((first[..., :1, :] - highest) * scale)
    second_scale = jnp.exp2((second[..., :1, :] - highest) * scale)
    sums = first[..., 1:, :] * first_scale + second[..., 1:, :] * second_scale
    return jnp.concatenate([highest, sums], axis=-2)


def routed(value, route):
    slots, cores = lax.axis_size("query"), lax.axis_size("target")
    pairs = []
    for slot in range(slots):
        for core in range(cores):
            to = route(slot, core)
            if to is not None:
                pairs.append((slot * cores + core, to[0] * cores + to[1]))
    return lax.ppermute(value, ("query", "target"), pairs)


def on_device(query_input, target_input, conv_weight, conv_bias):
    slot = lax.axis_index("query")
    core = lax.axis_index("target")
    slots = lax.axis_size("query")
    row_width = query_input.shape[1] // 2
    channels = conv_weight.shape[3]
    scale = LOG2E / math.sqrt(channels)
    first = core == 0

    def pick(on_first, on_second):
        return jnp.where(first, on_first, on_second)

    def swapped(value):
        return routed(value, lambda s, c: (s, 1 - c))

    far_rim, near_rim = rim_partials(query_input, target_input, conv_weight)
    near_rim = swapped(near_rim)
    far_rim = routed(far_rim, lambda s, c: ((s + 1) % slots, c)).astype(jnp.float32)
    far_rim = jnp.where(slot == 0, 0.0, far_rim)
    query_part, target_part = own_partials(query_input, target_input, conv_weight, conv_bias)
    odd = (target_part + pick(0.0, near_rim.astype(jnp.float32))).astype(jnp.bfloat16)
    handed = swapped(odd)
    odd_away = [
        routed(odd, lambda s, c: (s, 1) if c == 0 else ((s + 4 * hop) % slots, 0))
        for hop in range(1, max(2, slots // 4))
    ]
    whole = (pick(query_part, handed.astype(jnp.float32)) + far_rim).astype(jnp.bfloat16)
    even_away = [
        routed(whole, lambda s, c: (s ^ 2, 0) if c == 0 else ((s + 4 * hop) % slots, 1))
        for hop in range(1, max(2, slots // 4))
    ]
    corner = routed(whole, lambda s, c: (s ^ 3, 1) if c == 0 else (s, 0))
    beside = routed(whole, lambda s, c: (s ^ 1, 1) if c == 0 else (s, 0))

    members = [(whole, corner), (even_away[0], beside)]
    rows = [(corner, whole), (handed, odd)]
    states = [match(member, rows, lambda s, c: (2 * s, 2 * s + 1)) for member in members]
    for hop in range(1, slots // 4):
        away = swapped(pick(odd_away[hop - 1], even_away[hop - 1]))
        rows = [(odd_away[hop - 1], even_away[hop - 1]), (away, away)]

        def ids(s, c):
            source = lax.rem(s - 4 * hop + slots, slots)
            return 2 * source + 1 - c, 2 * source + c

        states = [match(member, rows, ids, state) for member, state in zip(members, states)]
    state, other = states
    corner_state = routed(state, lambda s, c: (s ^ 3, c))
    other = routed(other, lambda s, c: (s ^ (2 if c == 0 else 1), c))
    own = combined(pick(state, corner_state), other, scale)
    total = combined(own, swapped(own), scale)
    columns = jnp.arange(row_width, dtype=jnp.int32).astype(jnp.float32) * CELL
    flow_x = total[2] / total[1] - columns
    flow_y = total[3] / total[1] - slot.astype(jnp.float32) * CELL
    return jnp.stack([flow_x, flow_y]).reshape(2, 1, row_width)


def solution(mesh):
    placed = (
        P(("groups", "query"), None, None),
        P(("groups", "query", "target"), None, None),
        P(),
        P(),
    )
    return jax.shard_map(
        on_device,
        mesh=mesh,
        in_specs=placed,
        out_specs=P(None, ("groups", "query"), None),
        check_vma=False,
    )
```

```python
import functools
import math

import jax
import jax.numpy as jnp
from jax import lax
from jax.experimental import pallas as pl
from jax.experimental.pallas import tpu as pltpu
from jax.sharding import PartitionSpec as P

CELL = 0.0625
LOG2E = math.log2(math.e)
VMEM_LIMIT = 32 * 1024 * 1024
RIM_VMEM = (64 * 1024 - 10752) * 1024


def column_taps(row, stage):
    out_cols = row.shape[0] // 2
    stage[pl.ds(8, row.shape[0]), :] = row.astype(jnp.float32)
    return [
        stage[pl.ds(7 + tap, out_cols, stride=2), :].astype(jnp.bfloat16) for tap in range(3)
    ]


def tap_row_sum(row, weight_ref, tap_row, stage):
    taps = column_taps(row, stage)
    total = None
    for tap_col in range(3):
        term = jnp.dot(
            taps[tap_col], weight_ref[tap_row, tap_col], preferred_element_type=jnp.float32
        )
        total = term if total is None else total + term
    return total


def rim_kernel(
    query_hbm, target_hbm, weight_hbm, far_rim_ref, near_rim_ref, rows_ref, taps_ref, sems, *stages
):
    first = lax.axis_index("target") == 0
    last = query_hbm.shape[0] - 1
    copies = [
        pltpu.make_async_copy(weight_hbm.at[pl.ds(0, 1)], taps_ref, sems.at[2]),
        pltpu.make_async_copy(target_hbm.at[last], rows_ref.at[0], sems.at[0]),
        pltpu.make_async_copy(query_hbm.at[last], rows_ref.at[1], sems.at[1]),
    ]
    for copy in copies:
        copy.start()
    for stage in stages:
        stage[pl.ds(0, 8), :] = jnp.zeros((8, stage.shape[1]), jnp.float32)
    for copy in copies:
        copy.wait()
    target_rim = tap_row_sum(rows_ref[0], taps_ref, 0, stages[0])
    query_rim = tap_row_sum(rows_ref[1], taps_ref, 0, stages[1])
    near_rim_ref[...] = target_rim.astype(near_rim_ref.dtype)
    far_rim_ref[...] = jnp.where(first, query_rim, target_rim).astype(far_rim_ref.dtype)


def rim_partials(query_input, target_input, conv_weight):
    _, cols, channels = query_input.shape
    out_channels = conv_weight.shape[3]
    hbm = pl.BlockSpec(memory_space=pltpu.HBM)
    return pl.pallas_call(
        rim_kernel,
        out_shape=(jax.ShapeDtypeStruct((cols // 2, out_channels), jnp.bfloat16),) * 2,
        in_specs=[hbm] * 3,
        out_specs=(pl.BlockSpec(memory_space=pltpu.VMEM),) * 2,
        scratch_shapes=[
            pltpu.VMEM((2, cols, channels), jnp.bfloat16),
            pltpu.VMEM((1,) + conv_weight.shape[1:], jnp.bfloat16),
            pltpu.SemaphoreType.DMA((3,)),
        ]
        + [pltpu.VMEM((cols + 8, channels), jnp.float32)] * 2,
        compiler_params=pltpu.CompilerParams(vmem_limit_bytes=RIM_VMEM),
        name="rim_partials",
    )(query_input, target_input, conv_weight)


def own_kernel(query_ref, target_ref, weight_ref, bias_ref, query_out, target_out, *stages):
    for stage in stages:
        stage[pl.ds(0, 8), :] = jnp.zeros((8, stage.shape[1]), jnp.float32)
    pairs = ((target_ref, target_out), (query_ref, query_out))
    for which, (frame_ref, out_ref) in enumerate(pairs):
        total = bias_ref[...]
        for tap_row in (1, 2):
            total = total + tap_row_sum(
                frame_ref[tap_row - 1], weight_ref, tap_row, stages[2 * which + tap_row - 1]
            )
        out_ref[...] = total


def own_partials(query_input, target_input, conv_weight, conv_bias):
    _, cols, channels = query_input.shape
    out_channels = conv_weight.shape[3]
    part = jax.ShapeDtypeStruct((cols // 2, out_channels), jnp.float32)
    flops = 2 * 2 * 6 * (cols // 2) * channels * out_channels
    return pl.pallas_call(
        own_kernel,
        out_shape=(part, part),
        scratch_shapes=[pltpu.VMEM((cols + 8, channels), jnp.float32)] * 4,
        compiler_params=pltpu.CompilerParams(vmem_limit_bytes=VMEM_LIMIT),
        cost_estimate=pl.CostEstimate(flops=flops, bytes_accessed=1 << 22, transcendentals=0),
        name="own_partials",
    )(query_input, target_input, conv_weight, conv_bias.reshape(1, out_channels))


def merged(state, part, scale):
    top = jnp.maximum(state[0], part[0])
    keep = jnp.exp2((state[0] - top) * scale)
    gain = jnp.exp2((part[0] - top) * scale)
    return (top, *[old * keep + new * gain for old, new in zip(state[1:], part[1:])])


def match_kernel(members, carried, row_ids, *refs):
    core = lax.axis_index("target")
    refs = list(refs)
    query_pairs = [(refs.pop(0), refs.pop(0)) for _ in range(members)]
    target_pairs = [(refs.pop(0), refs.pop(0)) for _ in range(2)]
    state_refs = [refs.pop(0) for _ in range(members if carried else 0)]
    out_refs = [refs.pop(0) for _ in range(members)]
    lanes, channels = query_pairs[0][0].shape
    steps = target_pairs[0][0].shape[0] // 8
    scale = LOG2E / math.sqrt(channels)
    offset = lax.broadcasted_iota(jnp.int32, (8, lanes), 0).astype(jnp.float32)
    targets = [jnp.where(core == 0, one[...], two[...]) for one, two in target_pairs]
    for member, (one, two) in enumerate(query_pairs):
        queries = jnp.where(core == 0, one[...], two[...])
        for share in range(2):
            refs[2 * member + share][...] = lax.dot_general(
                targets[share],
                queries,
                (((1,), (1,)), ((), ())),
                preferred_element_type=jnp.float32,
            )
    for member, out_ref in enumerate(out_refs):
        state = None
        if carried:
            state = tuple(state_refs[member][pl.ds(i, 1), :] for i in range(4))
        for share, row_id in enumerate(row_ids(lax.axis_index("query"), core)):
            scores_ref = refs[2 * member + share]
            highest = scores_ref[pl.ds(0, 8), :]
            for step in range(1, steps):
                highest = jnp.maximum(highest, scores_ref[pl.ds(8 * step, 8), :])
            highest = jnp.max(highest, axis=0, keepdims=True)
            spread = jnp.broadcast_to(highest, (8, lanes))
            plain = jnp.zeros((8, lanes), jnp.float32)
            stacked = jnp.zeros((8, lanes), jnp.float32)
            for step in reversed(range(steps)):
                plain = plain + jnp.exp2((scores_ref[pl.ds(8 * step, 8), :] - spread) * scale)
                if step:
                    stacked = stacked + plain
            part_x = jnp.sum(8.0 * stacked + offset * plain, axis=0, keepdims=True) * CELL
            part_sum = jnp.sum(plain, axis=0, keepdims=True)
            part = (highest, part_sum, part_x, part_sum * (row_id.astype(jnp.float32) * CELL))
            state = part if state is None else merged(state, part, scale)
        out_ref[...] = jnp.concatenate(state, axis=0)


def match(members, targets, row_ids, states=()):
    lanes, channels = members[0][0].shape
    row_width = targets[0][0].shape[0]
    count = len(members)
    operands = [ref for pair in (*members, *targets) for ref in pair] + list(states)
    vmem = pl.BlockSpec(memory_space=pltpu.VMEM)
    return pl.pallas_call(
        functools.partial(match_kernel, count, bool(states), row_ids),
        out_shape=(jax.ShapeDtypeStruct((4, lanes), jnp.float32),) * count,
        in_specs=[vmem] * len(operands),
        out_specs=(vmem,) * count,
        scratch_shapes=[pltpu.VMEM((row_width, lanes), jnp.float32)] * (2 * count),
        compiler_params=pltpu.CompilerParams(vmem_limit_bytes=VMEM_LIMIT),
        cost_estimate=pl.CostEstimate(
            flops=4 * count * lanes * row_width * channels,
            bytes_accessed=1 << 22,
            transcendentals=2 * count * lanes * row_width,
        ),
        name="match",
    )(*operands)


def combined(first, second, scale):
    highest = jnp.maximum(first[..., :1, :], second[..., :1, :])
    first_scale = jnp.exp2((first[..., :1, :] - highest) * scale)
    second_scale = jnp.exp2((second[..., :1, :] - highest) * scale)
    sums = first[..., 1:, :] * first_scale + second[..., 1:, :] * second_scale
    return jnp.concatenate([highest, sums], axis=-2)


def routed(value, route):
    slots, cores = lax.axis_size("query"), lax.axis_size("target")
    pairs = []
    for slot in range(slots):
        for core in range(cores):
            to = route(slot, core)
            if to is not None:
                pairs.append((slot * cores + core, to[0] * cores + to[1]))
    return lax.ppermute(value, ("query", "target"), pairs)


def on_device(query_input, target_input, conv_weight, conv_bias):
    slot = lax.axis_index("query")
    core = lax.axis_index("target")
    slots = lax.axis_size("query")
    row_width = query_input.shape[1] // 2
    channels = conv_weight.shape[3]
    scale = LOG2E / math.sqrt(channels)
    first = core == 0

    def pick(on_first, on_second):
        return jnp.where(first, on_first, on_second)

    def swapped(value):
        return routed(value, lambda s, c: (s, 1 - c))

    far_rim, near_rim = rim_partials(query_input, target_input, conv_weight)
    near_rim = swapped(near_rim)
    far_rim = routed(far_rim, lambda s, c: ((s + 1) % slots, c)).astype(jnp.float32)
    far_rim = jnp.where(slot == 0, 0.0, far_rim)
    query_part, target_part = own_partials(query_input, target_input, conv_weight, conv_bias)
    odd = (target_part + pick(0.0, near_rim.astype(jnp.float32))).astype(jnp.bfloat16)
    handed = swapped(odd)
    odd_away = [
        routed(odd, lambda s, c: (s, 1) if c == 0 else ((s + 4 * hop) % slots, 0))
        for hop in range(1, max(2, slots // 4))
    ]
    whole = (pick(query_part, handed.astype(jnp.float32)) + far_rim).astype(jnp.bfloat16)
    even_away = [
        routed(whole, lambda s, c: (s ^ 1, 0) if c == 0 else ((s + 4 * hop) % slots, 1))
        for hop in range(1, max(2, slots // 4))
    ]
    below = routed(whole, lambda s, c: (s ^ 2, 1) if c == 0 else (s, 0))
    corner = routed(whole, lambda s, c: (s ^ 3, 1) if c == 0 else (s, 0))

    members = [(whole, below), (even_away[0], corner)]
    rows = [(below, whole), (handed, odd)]
    states = [match([member], rows, lambda s, c: (2 * s, 2 * s + 1))[0] for member in members]
    for hop in range(1, slots // 4):
        away = swapped(pick(odd_away[hop - 1], even_away[hop - 1]))
        rows = [(odd_away[hop - 1], even_away[hop - 1]), (away, away)]

        def ids(s, c):
            source = lax.rem(s - 4 * hop + slots, slots)
            return 2 * source + 1 - c, 2 * source + c

        states = match(members, rows, ids, states)
    state, other = states
    other = routed(other, lambda s, c: (s ^ (1 if c == 0 else 3), c))
    below_state = routed(state, lambda s, c: (s ^ (1 if c == 0 else 2), c))
    own = combined(pick(state, below_state), other, scale)
    total = combined(own, swapped(own), scale)
    columns = jnp.arange(row_width, dtype=jnp.int32).astype(jnp.float32) * CELL
    flow_x = total[2] / total[1] - columns
    flow_y = total[3] / total[1] - slot.astype(jnp.float32) * CELL
    return jnp.stack([flow_x, flow_y]).reshape(2, 1, row_width)


def solution(mesh):
    placed = (
        P(("groups", "query"), None, None),
        P(("groups", "query", "target"), None, None),
        P(),
        P(),
    )
    return jax.shard_map(
        on_device,
        mesh=mesh,
        in_specs=placed,
        out_specs=P(None, ("groups", "query"), None),
        check_vma=False,
    )
```

```python
import functools
import math

import jax
import jax.numpy as jnp
from jax import lax
from jax.experimental import pallas as pl
from jax.experimental.pallas import tpu as pltpu
from jax.sharding import PartitionSpec as P

CELL = 0.0625
LOG2E = math.log2(math.e)
VMEM_LIMIT = 32 * 1024 * 1024
RIM_VMEM = (64 * 1024 - 10752) * 1024


def column_taps(row, stage):
    out_cols = row.shape[0] // 2
    stage[pl.ds(8, row.shape[0]), :] = row.astype(jnp.float32)
    return [
        stage[pl.ds(7 + tap, out_cols, stride=2), :].astype(jnp.bfloat16) for tap in range(3)
    ]


def tap_row_sum(row, weight_ref, tap_row, stage):
    taps = column_taps(row, stage)
    total = None
    for tap_col in range(3):
        term = jnp.dot(
            taps[tap_col], weight_ref[tap_row, tap_col], preferred_element_type=jnp.float32
        )
        total = term if total is None else total + term
    return total


def rim_kernel(
    query_hbm, target_hbm, weight_hbm, far_rim_ref, near_rim_ref, rows_ref, taps_ref, sems, *stages
):
    first = lax.axis_index("target") == 0
    last = query_hbm.shape[0] - 1
    copies = [
        pltpu.make_async_copy(weight_hbm.at[pl.ds(0, 1)], taps_ref, sems.at[2]),
        pltpu.make_async_copy(target_hbm.at[last], rows_ref.at[0], sems.at[0]),
        pltpu.make_async_copy(query_hbm.at[last], rows_ref.at[1], sems.at[1]),
    ]
    for copy in copies:
        copy.start()
    for stage in stages:
        stage[pl.ds(0, 8), :] = jnp.zeros((8, stage.shape[1]), jnp.float32)
    for copy in copies:
        copy.wait()
    target_rim = tap_row_sum(rows_ref[0], taps_ref, 0, stages[0])
    query_rim = tap_row_sum(rows_ref[1], taps_ref, 0, stages[1])
    near_rim_ref[...] = target_rim.astype(near_rim_ref.dtype)
    far_rim_ref[...] = jnp.where(first, query_rim, target_rim).astype(far_rim_ref.dtype)


def rim_partials(query_input, target_input, conv_weight):
    _, cols, channels = query_input.shape
    out_channels = conv_weight.shape[3]
    hbm = pl.BlockSpec(memory_space=pltpu.HBM)
    return pl.pallas_call(
        rim_kernel,
        out_shape=(jax.ShapeDtypeStruct((cols // 2, out_channels), jnp.bfloat16),) * 2,
        in_specs=[hbm] * 3,
        out_specs=(pl.BlockSpec(memory_space=pltpu.VMEM),) * 2,
        scratch_shapes=[
            pltpu.VMEM((2, cols, channels), jnp.bfloat16),
            pltpu.VMEM((1,) + conv_weight.shape[1:], jnp.bfloat16),
            pltpu.SemaphoreType.DMA((3,)),
        ]
        + [pltpu.VMEM((cols + 8, channels), jnp.float32)] * 2,
        compiler_params=pltpu.CompilerParams(vmem_limit_bytes=RIM_VMEM),
        name="rim_partials",
    )(query_input, target_input, conv_weight)


def own_kernel(query_ref, target_ref, weight_ref, bias_ref, query_out, target_out, *stages):
    for stage in stages:
        stage[pl.ds(0, 8), :] = jnp.zeros((8, stage.shape[1]), jnp.float32)
    pairs = ((target_ref, target_out), (query_ref, query_out))
    for which, (frame_ref, out_ref) in enumerate(pairs):
        total = bias_ref[...]
        for tap_row in (1, 2):
            total = total + tap_row_sum(
                frame_ref[tap_row - 1], weight_ref, tap_row, stages[2 * which + tap_row - 1]
            )
        out_ref[...] = total


def own_partials(query_input, target_input, conv_weight, conv_bias):
    _, cols, channels = query_input.shape
    out_channels = conv_weight.shape[3]
    part = jax.ShapeDtypeStruct((cols // 2, out_channels), jnp.float32)
    flops = 2 * 2 * 6 * (cols // 2) * channels * out_channels
    return pl.pallas_call(
        own_kernel,
        out_shape=(part, part),
        scratch_shapes=[pltpu.VMEM((cols + 8, channels), jnp.float32)] * 4,
        compiler_params=pltpu.CompilerParams(vmem_limit_bytes=VMEM_LIMIT),
        cost_estimate=pl.CostEstimate(flops=flops, bytes_accessed=1 << 22, transcendentals=0),
        name="own_partials",
    )(query_input, target_input, conv_weight, conv_bias.reshape(1, out_channels))


def merged(state, part, scale):
    top = jnp.maximum(state[0], part[0])
    keep = jnp.exp2((state[0] - top) * scale)
    gain = jnp.exp2((part[0] - top) * scale)
    return (top, *[old * keep + new * gain for old, new in zip(state[1:], part[1:])])


def match_kernel(members, carried, row_ids, *refs):
    core = lax.axis_index("target")
    refs = list(refs)
    query_pairs = [(refs.pop(0), refs.pop(0)) for _ in range(members)]
    target_pairs = [(refs.pop(0), refs.pop(0)) for _ in range(2)]
    state_refs = [refs.pop(0) for _ in range(members if carried else 0)]
    out_refs = [refs.pop(0) for _ in range(members)]
    lanes, channels = query_pairs[0][0].shape
    steps = target_pairs[0][0].shape[0] // 8
    scale = LOG2E / math.sqrt(channels)
    offset = lax.broadcasted_iota(jnp.int32, (8, lanes), 0).astype(jnp.float32)
    targets = [jnp.where(core == 0, one[...], two[...]) for one, two in target_pairs]
    for member, (one, two) in enumerate(query_pairs):
        queries = jnp.where(core == 0, one[...], two[...])
        for share in range(2):
            refs[2 * member + share][...] = lax.dot_general(
                targets[share],
                queries,
                (((1,), (1,)), ((), ())),
                preferred_element_type=jnp.float32,
            )
    for member, out_ref in enumerate(out_refs):
        state = None
        if carried:
            state = tuple(state_refs[member][pl.ds(i, 1), :] for i in range(4))
        for share, row_id in enumerate(row_ids(lax.axis_index("query"), core)):
            scores_ref = refs[2 * member + share]
            highest = scores_ref[pl.ds(0, 8), :]
            for step in range(1, steps):
                highest = jnp.maximum(highest, scores_ref[pl.ds(8 * step, 8), :])
            highest = jnp.max(highest, axis=0, keepdims=True)
            spread = jnp.broadcast_to(highest, (8, lanes))
            plain = jnp.zeros((8, lanes), jnp.float32)
            stacked = jnp.zeros((8, lanes), jnp.float32)
            for step in reversed(range(steps)):
                plain = plain + jnp.exp2((scores_ref[pl.ds(8 * step, 8), :] - spread) * scale)
                if step:
                    stacked = stacked + plain
            part_x = jnp.sum(8.0 * stacked + offset * plain, axis=0, keepdims=True) * CELL
            part_sum = jnp.sum(plain, axis=0, keepdims=True)
            part = (highest, part_sum, part_x, part_sum * (row_id.astype(jnp.float32) * CELL))
            state = part if state is None else merged(state, part, scale)
        out_ref[...] = jnp.concatenate(state, axis=0)


def match(members, targets, row_ids, states=()):
    lanes, channels = members[0][0].shape
    row_width = targets[0][0].shape[0]
    count = len(members)
    operands = [ref for pair in (*members, *targets) for ref in pair] + list(states)
    vmem = pl.BlockSpec(memory_space=pltpu.VMEM)
    return pl.pallas_call(
        functools.partial(match_kernel, count, bool(states), row_ids),
        out_shape=(jax.ShapeDtypeStruct((4, lanes), jnp.float32),) * count,
        in_specs=[vmem] * len(operands),
        out_specs=(vmem,) * count,
        scratch_shapes=[pltpu.VMEM((row_width, lanes), jnp.float32)] * (2 * count),
        compiler_params=pltpu.CompilerParams(vmem_limit_bytes=VMEM_LIMIT),
        cost_estimate=pl.CostEstimate(
            flops=4 * count * lanes * row_width * channels,
            bytes_accessed=1 << 22,
            transcendentals=2 * count * lanes * row_width,
        ),
        name="match",
    )(*operands)


def combined(first, second, scale):
    highest = jnp.maximum(first[..., :1, :], second[..., :1, :])
    first_scale = jnp.exp2((first[..., :1, :] - highest) * scale)
    second_scale = jnp.exp2((second[..., :1, :] - highest) * scale)
    sums = first[..., 1:, :] * first_scale + second[..., 1:, :] * second_scale
    return jnp.concatenate([highest, sums], axis=-2)


def routed(value, route):
    slots, cores = lax.axis_size("query"), lax.axis_size("target")
    pairs = []
    for slot in range(slots):
        for core in range(cores):
            to = route(slot, core)
            if to is not None:
                pairs.append((slot * cores + core, to[0] * cores + to[1]))
    return lax.ppermute(value, ("query", "target"), pairs)


def on_device(query_input, target_input, conv_weight, conv_bias):
    slot = lax.axis_index("query")
    core = lax.axis_index("target")
    slots = lax.axis_size("query")
    row_width = query_input.shape[1] // 2
    channels = conv_weight.shape[3]
    scale = LOG2E / math.sqrt(channels)
    first = core == 0

    def pick(on_first, on_second):
        return jnp.where(first, on_first, on_second)

    def swapped(value):
        return routed(value, lambda s, c: (s, 1 - c))

    far_rim, near_rim = rim_partials(query_input, target_input, conv_weight)
    near_rim = swapped(near_rim)
    far_rim = routed(far_rim, lambda s, c: ((s + 1) % slots, c)).astype(jnp.float32)
    far_rim = jnp.where(slot == 0, 0.0, far_rim)
    query_part, target_part = own_partials(query_input, target_input, conv_weight, conv_bias)
    odd = (target_part + pick(0.0, near_rim.astype(jnp.float32))).astype(jnp.bfloat16)
    handed = swapped(odd)
    odd_away = [
        routed(odd, lambda s, c: (s, 1) if c == 0 else ((s + 4 * hop) % slots, 0))
        for hop in range(1, max(2, slots // 4))
    ]
    whole = (pick(query_part, handed.astype(jnp.float32)) + far_rim).astype(jnp.bfloat16)
    even_away = [
        routed(whole, lambda s, c: (s ^ 1, 0) if c == 0 else ((s + 4 * hop) % slots, 1))
        for hop in range(1, max(2, slots // 4))
    ]
    below = routed(whole, lambda s, c: (s ^ 2, 1) if c == 0 else (s, 0))
    corner = routed(whole, lambda s, c: (s ^ 3, 1) if c == 0 else (s, 0))

    members = [(whole, corner), (even_away[0], below)]
    rows = [(corner, whole), (handed, odd)]
    states = [match([member], rows, lambda s, c: (2 * s, 2 * s + 1))[0] for member in members]
    for hop in range(1, slots // 4):
        away = swapped(pick(odd_away[hop - 1], even_away[hop - 1]))
        rows = [(odd_away[hop - 1], even_away[hop - 1]), (away, away)]

        def ids(s, c):
            source = lax.rem(s - 4 * hop + slots, slots)
            return 2 * source + 1 - c, 2 * source + c

        states = match(members, rows, ids, states)
    state, other = states
    corner_state = routed(state, lambda s, c: (s ^ (1 if c == 0 else 3), c))
    near_state = routed(other, lambda s, c: (s ^ (1 if c == 0 else 2), c))
    own = combined(pick(state, corner_state), near_state, scale)
    total = combined(own, swapped(own), scale)
    columns = jnp.arange(row_width, dtype=jnp.int32).astype(jnp.float32) * CELL
    flow_x = total[2] / total[1] - columns
    flow_y = total[3] / total[1] - slot.astype(jnp.float32) * CELL
    return jnp.stack([flow_x, flow_y]).reshape(2, 1, row_width)


def solution(mesh):
    placed = (
        P(("groups", "query"), None, None),
        P(("groups", "query", "target"), None, None),
        P(),
        P(),
    )
    return jax.shard_map(
        on_device,
        mesh=mesh,
        in_specs=placed,
        out_specs=P(None, ("groups", "query"), None),
        check_vma=False,
    )
```

```python
import functools
import math

import jax
import jax.numpy as jnp
from jax import lax
from jax.experimental import pallas as pl
from jax.experimental.pallas import tpu as pltpu
from jax.sharding import PartitionSpec as P

CELL = 0.0625
LOG2E = math.log2(math.e)
VMEM_LIMIT = 32 * 1024 * 1024
RIM_VMEM = (64 * 1024 - 10944) * 1024


def column_taps(row, stage):
    out_cols = row.shape[0] // 2
    stage[pl.ds(8, row.shape[0]), :] = row.astype(jnp.float32)
    return [
        stage[pl.ds(7 + tap, out_cols, stride=2), :].astype(jnp.bfloat16) for tap in range(3)
    ]


def tap_row_sum(row, weight_ref, tap_row, stage):
    taps = column_taps(row, stage)
    total = None
    for tap_col in range(3):
        term = jnp.dot(
            taps[tap_col], weight_ref[tap_row, tap_col], preferred_element_type=jnp.float32
        )
        total = term if total is None else total + term
    return total


def rim_kernel(
    query_hbm, target_hbm, weight_hbm, far_rim_ref, near_rim_ref, rows_ref, taps_ref, sems, *stages
):
    first = lax.axis_index("target") == 0
    last = query_hbm.shape[0] - 1
    copies = [
        pltpu.make_async_copy(weight_hbm.at[pl.ds(0, 1)], taps_ref, sems.at[2]),
        pltpu.make_async_copy(target_hbm.at[last], rows_ref.at[0], sems.at[0]),
        pltpu.make_async_copy(query_hbm.at[last], rows_ref.at[1], sems.at[1]),
    ]
    for copy in copies:
        copy.start()
    for stage in stages:
        stage[pl.ds(0, 8), :] = jnp.zeros((8, stage.shape[1]), jnp.float32)
    for copy in copies:
        copy.wait()
    target_rim = tap_row_sum(rows_ref[0], taps_ref, 0, stages[0])
    query_rim = tap_row_sum(rows_ref[1], taps_ref, 0, stages[1])
    near_rim_ref[...] = target_rim.astype(near_rim_ref.dtype)
    far_rim_ref[...] = jnp.where(first, query_rim, target_rim).astype(far_rim_ref.dtype)


def rim_partials(query_input, target_input, conv_weight):
    _, cols, channels = query_input.shape
    out_channels = conv_weight.shape[3]
    hbm = pl.BlockSpec(memory_space=pltpu.HBM)
    return pl.pallas_call(
        rim_kernel,
        out_shape=(jax.ShapeDtypeStruct((cols // 2, out_channels), jnp.float32),) * 2,
        in_specs=[hbm] * 3,
        out_specs=(pl.BlockSpec(memory_space=pltpu.VMEM),) * 2,
        scratch_shapes=[
            pltpu.VMEM((2, cols, channels), jnp.bfloat16),
            pltpu.VMEM((1,) + conv_weight.shape[1:], jnp.bfloat16),
            pltpu.SemaphoreType.DMA((3,)),
        ]
        + [pltpu.VMEM((cols + 8, channels), jnp.float32)] * 2,
        compiler_params=pltpu.CompilerParams(vmem_limit_bytes=RIM_VMEM),
        name="rim_partials",
    )(query_input, target_input, conv_weight)


def own_kernel(query_ref, target_ref, weight_ref, bias_ref, query_out, target_out, *stages):
    for stage in stages:
        stage[pl.ds(0, 8), :] = jnp.zeros((8, stage.shape[1]), jnp.float32)
    pairs = ((target_ref, target_out), (query_ref, query_out))
    for which, (frame_ref, out_ref) in enumerate(pairs):
        total = bias_ref[...]
        for tap_row in (1, 2):
            total = total + tap_row_sum(
                frame_ref[tap_row - 1], weight_ref, tap_row, stages[2 * which + tap_row - 1]
            )
        out_ref[...] = total


def own_partials(query_input, target_input, conv_weight, conv_bias):
    _, cols, channels = query_input.shape
    out_channels = conv_weight.shape[3]
    part = jax.ShapeDtypeStruct((cols // 2, out_channels), jnp.float32)
    flops = 2 * 2 * 6 * (cols // 2) * channels * out_channels
    return pl.pallas_call(
        own_kernel,
        out_shape=(part, part),
        scratch_shapes=[pltpu.VMEM((cols + 8, channels), jnp.float32)] * 4,
        compiler_params=pltpu.CompilerParams(vmem_limit_bytes=VMEM_LIMIT),
        cost_estimate=pl.CostEstimate(flops=flops, bytes_accessed=1 << 22, transcendentals=0),
        name="own_partials",
    )(query_input, target_input, conv_weight, conv_bias.reshape(1, out_channels))


def merged(state, part, scale):
    top = jnp.maximum(state[0], part[0])
    keep = jnp.exp2((state[0] - top) * scale)
    gain = jnp.exp2((part[0] - top) * scale)
    return (top, *[old * keep + new * gain for old, new in zip(state[1:], part[1:])])


def match_kernel(members, carried, row_ids, *refs):
    core = lax.axis_index("target")
    refs = list(refs)
    query_pairs = [(refs.pop(0), refs.pop(0)) for _ in range(members)]
    target_pairs = [(refs.pop(0), refs.pop(0)) for _ in range(2)]
    state_refs = [refs.pop(0) for _ in range(members if carried else 0)]
    out_refs = [refs.pop(0) for _ in range(members)]
    lanes, channels = query_pairs[0][0].shape
    steps = target_pairs[0][0].shape[0] // 8
    scale = LOG2E / math.sqrt(channels)
    offset = lax.broadcasted_iota(jnp.int32, (8, lanes), 0).astype(jnp.float32)
    targets = [jnp.where(core == 0, one[...], two[...]) for one, two in target_pairs]
    for member, (one, two) in enumerate(query_pairs):
        queries = jnp.where(core == 0, one[...], two[...])
        for share in range(2):
            refs[2 * member + share][...] = lax.dot_general(
                targets[share],
                queries,
                (((1,), (1,)), ((), ())),
                preferred_element_type=jnp.float32,
            )
    for member, out_ref in enumerate(out_refs):
        state = None
        if carried:
            state = tuple(state_refs[member][pl.ds(i, 1), :] for i in range(4))
        for share, row_id in enumerate(row_ids(lax.axis_index("query"), core)):
            scores_ref = refs[2 * member + share]
            highest = scores_ref[pl.ds(0, 8), :]
            for step in range(1, steps):
                highest = jnp.maximum(highest, scores_ref[pl.ds(8 * step, 8), :])
            highest = jnp.max(highest, axis=0, keepdims=True)
            spread = jnp.broadcast_to(highest, (8, lanes))
            plain = jnp.zeros((8, lanes), jnp.float32)
            stacked = jnp.zeros((8, lanes), jnp.float32)
            for step in reversed(range(steps)):
                plain = plain + jnp.exp2((scores_ref[pl.ds(8 * step, 8), :] - spread) * scale)
                if step:
                    stacked = stacked + plain
            part_x = jnp.sum(8.0 * stacked + offset * plain, axis=0, keepdims=True) * CELL
            part_sum = jnp.sum(plain, axis=0, keepdims=True)
            part = (highest, part_sum, part_x, part_sum * (row_id.astype(jnp.float32) * CELL))
            state = part if state is None else merged(state, part, scale)
        out_ref[...] = jnp.concatenate(state, axis=0)


def match(members, targets, row_ids, states=()):
    lanes, channels = members[0][0].shape
    row_width = targets[0][0].shape[0]
    count = len(members)
    operands = [ref for pair in (*members, *targets) for ref in pair] + list(states)
    vmem = pl.BlockSpec(memory_space=pltpu.VMEM)
    return pl.pallas_call(
        functools.partial(match_kernel, count, bool(states), row_ids),
        out_shape=(jax.ShapeDtypeStruct((4, lanes), jnp.float32),) * count,
        in_specs=[vmem] * len(operands),
        out_specs=(vmem,) * count,
        scratch_shapes=[pltpu.VMEM((row_width, lanes), jnp.float32)] * (2 * count),
        compiler_params=pltpu.CompilerParams(vmem_limit_bytes=VMEM_LIMIT),
        cost_estimate=pl.CostEstimate(
            flops=4 * count * lanes * row_width * channels,
            bytes_accessed=1 << 22,
            transcendentals=2 * count * lanes * row_width,
        ),
        name="match",
    )(*operands)


def combined(first, second, scale):
    highest = jnp.maximum(first[..., :1, :], second[..., :1, :])
    first_scale = jnp.exp2((first[..., :1, :] - highest) * scale)
    second_scale = jnp.exp2((second[..., :1, :] - highest) * scale)
    sums = first[..., 1:, :] * first_scale + second[..., 1:, :] * second_scale
    return jnp.concatenate([highest, sums], axis=-2)


def routed(value, route):
    slots, cores = lax.axis_size("query"), lax.axis_size("target")
    pairs = []
    for slot in range(slots):
        for core in range(cores):
            to = route(slot, core)
            if to is not None:
                pairs.append((slot * cores + core, to[0] * cores + to[1]))
    return lax.ppermute(value, ("query", "target"), pairs)


def on_device(query_input, target_input, conv_weight, conv_bias):
    slot = lax.axis_index("query")
    core = lax.axis_index("target")
    slots = lax.axis_size("query")
    row_width = query_input.shape[1] // 2
    channels = conv_weight.shape[3]
    scale = LOG2E / math.sqrt(channels)
    first = core == 0

    def pick(on_first, on_second):
        return jnp.where(first, on_first, on_second)

    def swapped(value):
        return routed(value, lambda s, c: (s, 1 - c))

    far_rim, near_rim = rim_partials(query_input, target_input, conv_weight)
    near_rim = swapped(near_rim)
    far_rim = routed(far_rim, lambda s, c: ((s + 1) % slots, c))
    far_rim = jnp.where(slot == 0, 0.0, far_rim)
    query_part, target_part = own_partials(query_input, target_input, conv_weight, conv_bias)
    odd = (target_part + near_rim).astype(jnp.bfloat16)
    handed = swapped(pick(target_part, odd.astype(jnp.float32)))
    odd_away = [
        routed(odd, lambda s, c: (s, 1) if c == 0 else ((s + 4 * hop) % slots, 0))
        for hop in range(1, max(2, slots // 4))
    ]
    whole = (pick(query_part, handed) + far_rim).astype(jnp.bfloat16)
    handed = handed.astype(jnp.bfloat16)
    even_away = [
        routed(whole, lambda s, c: (s ^ 1, 0) if c == 0 else ((s + 4 * hop) % slots, 1))
        for hop in range(1, max(2, slots // 4))
    ]
    below = routed(whole, lambda s, c: (s ^ 2, 1) if c == 0 else (s, 0))
    corner = routed(whole, lambda s, c: (s ^ 3, 1) if c == 0 else (s, 0))

    members = [(whole, corner), (even_away[0], below)]
    rows = [(corner, whole), (handed, odd)]
    states = [match([member], rows, lambda s, c: (2 * s, 2 * s + 1))[0] for member in members]
    for hop in range(1, slots // 4):
        away = swapped(pick(odd_away[hop - 1], even_away[hop - 1]))
        rows = [(odd_away[hop - 1], even_away[hop - 1]), (away, away)]

        def ids(s, c):
            source = lax.rem(s - 4 * hop + slots, slots)
            return 2 * source + 1 - c, 2 * source + c

        states = match(members, rows, ids, states)
    state, other = states
    corner_state = routed(state, lambda s, c: (s ^ (1 if c == 0 else 3), c))
    near_state = routed(other, lambda s, c: (s ^ (1 if c == 0 else 2), c))
    own = combined(pick(state, corner_state), near_state, scale)
    total = combined(own, swapped(own), scale)
    columns = jnp.arange(row_width, dtype=jnp.int32).astype(jnp.float32) * CELL
    flow_x = total[2] / total[1] - columns
    flow_y = total[3] / total[1] - slot.astype(jnp.float32) * CELL
    return jnp.stack([flow_x, flow_y]).reshape(2, 1, row_width)


def solution(mesh):
    placed = (
        P(("groups", "query"), None, None),
        P(("groups", "query", "target"), None, None),
        P(),
        P(),
    )
    return jax.shard_map(
        on_device,
        mesh=mesh,
        in_specs=placed,
        out_specs=P(None, ("groups", "query"), None),
        check_vma=False,
    )
```

```python
import functools
import math

import jax
import jax.numpy as jnp
from jax import lax
from jax.experimental import pallas as pl
from jax.experimental.pallas import tpu as pltpu
from jax.sharding import PartitionSpec as P

CELL = 0.0625
LOG2E = math.log2(math.e)
VMEM_LIMIT = 32 * 1024 * 1024
ROOT_SCALE = 0.1875
RIM_VMEM = (64 * 1024 - 10944) * 1024


def column_taps(row, stage):
    out_cols = row.shape[0] // 2
    stage[pl.ds(8, row.shape[0]), :] = row.astype(jnp.float32)
    return [
        stage[pl.ds(7 + tap, out_cols, stride=2), :].astype(jnp.bfloat16) for tap in range(3)
    ]


def tap_row_sum(row, weight_ref, tap_row, stage):
    taps = column_taps(row, stage)
    total = None
    for tap_col in range(3):
        term = jnp.dot(
            taps[tap_col], weight_ref[tap_row, tap_col], preferred_element_type=jnp.float32
        )
        total = term if total is None else total + term
    return total


def rim_kernel(
    query_hbm, target_hbm, weight_hbm, far_rim_ref, near_rim_ref, rows_ref, taps_ref, sems, *stages
):
    first = lax.axis_index("target") == 0
    last = query_hbm.shape[0] - 1
    copies = [
        pltpu.make_async_copy(weight_hbm.at[pl.ds(0, 1)], taps_ref, sems.at[2]),
        pltpu.make_async_copy(target_hbm.at[last], rows_ref.at[0], sems.at[0]),
        pltpu.make_async_copy(query_hbm.at[last], rows_ref.at[1], sems.at[1]),
    ]
    for copy in copies:
        copy.start()
    for stage in stages:
        stage[pl.ds(0, 8), :] = jnp.zeros((8, stage.shape[1]), jnp.float32)
    for copy in copies:
        copy.wait()
    target_rim = tap_row_sum(rows_ref[0], taps_ref, 0, stages[0])
    query_rim = tap_row_sum(rows_ref[1], taps_ref, 0, stages[1])
    near_rim_ref[...] = target_rim.astype(near_rim_ref.dtype)
    far_rim_ref[...] = jnp.where(first, query_rim, target_rim).astype(far_rim_ref.dtype)


def rim_partials(query_input, target_input, conv_weight):
    _, cols, channels = query_input.shape
    out_channels = conv_weight.shape[3]
    hbm = pl.BlockSpec(memory_space=pltpu.HBM)
    return pl.pallas_call(
        rim_kernel,
        out_shape=(jax.ShapeDtypeStruct((cols // 2, out_channels), jnp.float32),) * 2,
        in_specs=[hbm] * 3,
        out_specs=(pl.BlockSpec(memory_space=pltpu.VMEM),) * 2,
        scratch_shapes=[
            pltpu.VMEM((2, cols, channels), jnp.bfloat16),
            pltpu.VMEM((1,) + conv_weight.shape[1:], jnp.bfloat16),
            pltpu.SemaphoreType.DMA((3,)),
        ]
        + [pltpu.VMEM((cols + 8, channels), jnp.float32)] * 2,
        compiler_params=pltpu.CompilerParams(vmem_limit_bytes=RIM_VMEM),
        name="rim_partials",
    )(query_input, target_input, conv_weight)


def own_kernel(
    query_ref, target_ref, weight_ref, bias_ref, query_out, target_out, upper_ref, lower_ref, *stages
):
    for stage in stages:
        stage[pl.ds(0, 8), :] = jnp.zeros((8, stage.shape[1]), jnp.float32)
    pairs = ((target_ref, target_out), (query_ref, query_out))
    for which, (frame_ref, out_ref) in enumerate(pairs):
        total = bias_ref[...]
        for tap_row in (1, 2):
            total = total + tap_row_sum(
                frame_ref[tap_row - 1], weight_ref, tap_row, stages[2 * which + tap_row - 1]
            )
        out_ref[...] = total
        if which == 0:
            upper = total.astype(jnp.bfloat16)
            upper_ref[...] = upper
            lower_ref[...] = (total - upper.astype(jnp.float32)).astype(jnp.bfloat16)


def own_partials(query_input, target_input, conv_weight, conv_bias):
    _, cols, channels = query_input.shape
    out_channels = conv_weight.shape[3]
    part = jax.ShapeDtypeStruct((cols // 2, out_channels), jnp.float32)
    half = jax.ShapeDtypeStruct((cols // 2, out_channels), jnp.bfloat16)
    flops = 2 * 2 * 6 * (cols // 2) * channels * out_channels
    return pl.pallas_call(
        own_kernel,
        out_shape=(part, part, half, half),
        scratch_shapes=[pltpu.VMEM((cols + 8, channels), jnp.float32)] * 4,
        compiler_params=pltpu.CompilerParams(vmem_limit_bytes=VMEM_LIMIT),
        cost_estimate=pl.CostEstimate(flops=flops, bytes_accessed=1 << 22, transcendentals=0),
        name="own_partials",
    )(query_input, target_input, conv_weight, conv_bias.reshape(1, out_channels))


def merged(state, part, scale):
    top = jnp.maximum(state[0], part[0])
    keep = jnp.exp2((state[0] - top) * scale)
    gain = jnp.exp2((part[0] - top) * scale)
    return (top, *[old * keep + new * gain for old, new in zip(state[1:], part[1:])])


def match_kernel(members, carried, row_ids, *refs):
    core = lax.axis_index("target")
    refs = list(refs)
    query_pairs = [(refs.pop(0), refs.pop(0)) for _ in range(members)]
    target_pairs = [(refs.pop(0), refs.pop(0)) for _ in range(2)]
    state_refs = [refs.pop(0) for _ in range(members if carried else 0)]
    out_refs = [refs.pop(0) for _ in range(members)]
    lanes, channels = query_pairs[0][0].shape
    steps = target_pairs[0][0].shape[0] // 8
    scale = LOG2E / math.sqrt(channels)
    offset = lax.broadcasted_iota(jnp.int32, (8, lanes), 0).astype(jnp.float32)
    targets = [jnp.where(core == 0, one[...], two[...]) for one, two in target_pairs]
    for member, (one, two) in enumerate(query_pairs):
        queries = jnp.where(core == 0, one[...], two[...])
        for share in range(2):
            refs[2 * member + share][...] = lax.dot_general(
                targets[share],
                queries,
                (((1,), (1,)), ((), ())),
                preferred_element_type=jnp.float32,
            )
    for member, out_ref in enumerate(out_refs):
        state = None
        if carried:
            state = tuple(state_refs[member][pl.ds(i, 1), :] for i in range(4))
        for share, row_id in enumerate(row_ids(lax.axis_index("query"), core)):
            scores_ref = refs[2 * member + share]
            highest = scores_ref[pl.ds(0, 8), :]
            for step in range(1, steps):
                highest = jnp.maximum(highest, scores_ref[pl.ds(8 * step, 8), :])
            highest = jnp.max(highest, axis=0, keepdims=True)
            spread = jnp.broadcast_to(highest, (8, lanes))
            plain = jnp.zeros((8, lanes), jnp.float32)
            stacked = jnp.zeros((8, lanes), jnp.float32)
            for step in reversed(range(steps)):
                plain = plain + jnp.exp2((scores_ref[pl.ds(8 * step, 8), :] - spread) * scale)
                if step:
                    stacked = stacked + plain
            part_x = jnp.sum(8.0 * stacked + offset * plain, axis=0, keepdims=True) * CELL
            part_sum = jnp.sum(plain, axis=0, keepdims=True)
            part = (highest, part_sum, part_x, part_sum * (row_id.astype(jnp.float32) * CELL))
            state = part if state is None else merged(state, part, scale)
        out_ref[...] = jnp.concatenate(state, axis=0)


def match(members, targets, row_ids, states=()):
    lanes, channels = members[0][0].shape
    row_width = targets[0][0].shape[0]
    count = len(members)
    operands = [ref for pair in (*members, *targets) for ref in pair] + list(states)
    vmem = pl.BlockSpec(memory_space=pltpu.VMEM)
    return pl.pallas_call(
        functools.partial(match_kernel, count, bool(states), row_ids),
        out_shape=(jax.ShapeDtypeStruct((4, lanes), jnp.float32),) * count,
        in_specs=[vmem] * len(operands),
        out_specs=(vmem,) * count,
        scratch_shapes=[pltpu.VMEM((row_width, lanes), jnp.float32)] * (2 * count),
        compiler_params=pltpu.CompilerParams(vmem_limit_bytes=VMEM_LIMIT),
        cost_estimate=pl.CostEstimate(
            flops=4 * count * lanes * row_width * channels,
            bytes_accessed=1 << 22,
            transcendentals=2 * count * lanes * row_width,
        ),
        name="match",
    )(*operands)


def combined(first, second, scale):
    highest = jnp.maximum(first[..., :1, :], second[..., :1, :])
    first_scale = jnp.exp2((first[..., :1, :] - highest) * scale)
    second_scale = jnp.exp2((second[..., :1, :] - highest) * scale)
    sums = first[..., 1:, :] * first_scale + second[..., 1:, :] * second_scale
    return jnp.concatenate([highest, sums], axis=-2)


def routed(value, route):
    slots, cores = lax.axis_size("query"), lax.axis_size("target")
    pairs = []
    for slot in range(slots):
        for core in range(cores):
            to = route(slot, core)
            if to is not None:
                pairs.append((slot * cores + core, to[0] * cores + to[1]))
    return lax.ppermute(value, ("query", "target"), pairs)


def squared(value):
    return (value * jnp.abs(value) * (ROOT_SCALE * ROOT_SCALE)).astype(jnp.float16)


def rooted(square):
    square = square.astype(jnp.float32)
    root = jnp.sqrt(jnp.abs(square)) * (1.0 / ROOT_SCALE)
    return jnp.where(square < 0, -root, root)


def on_device(query_input, target_input, conv_weight, conv_bias):
    slot = lax.axis_index("query")
    core = lax.axis_index("target")
    slots = lax.axis_size("query")
    row_width = query_input.shape[1] // 2
    channels = conv_weight.shape[3]
    scale = LOG2E / math.sqrt(channels)
    first = core == 0

    def pick(on_first, on_second):
        return jnp.where(first, on_first, on_second)

    def swapped(value):
        return routed(value, lambda s, c: (s, 1 - c))

    far_rim, near_rim = rim_partials(query_input, target_input, conv_weight)
    near_rim = swapped(near_rim)
    far_rim, conv_bias = lax.optimization_barrier((squared(far_rim), conv_bias))
    far_rim = routed(far_rim, lambda s, c: ((s + 1) % slots, c))
    far_rim = jnp.where(slot == 0, 0.0, rooted(far_rim))
    near_rim, conv_bias = lax.optimization_barrier((near_rim, conv_bias))
    query_part, target_part, upper, lower = own_partials(
        query_input, target_input, conv_weight, conv_bias
    )
    odd = (target_part + near_rim).astype(jnp.bfloat16)
    handed = swapped(pick(upper, odd))
    rest = swapped(lower)
    odd_away = [
        routed(odd, lambda s, c: (s, 1) if c == 0 else ((s + 4 * hop) % slots, 0))
        for hop in range(1, max(2, slots // 4))
    ]
    unfinished = handed.astype(jnp.float32) + rest.astype(jnp.float32)
    whole = (pick(query_part, unfinished) + far_rim).astype(jnp.bfloat16)
    even_away = [
        routed(whole, lambda s, c: (s ^ 1, 0) if c == 0 else ((s + 4 * hop) % slots, 1))
        for hop in range(1, max(2, slots // 4))
    ]
    below = routed(whole, lambda s, c: (s ^ 2, 1) if c == 0 else (s, 0))
    corner = routed(whole, lambda s, c: (s ^ 3, 1) if c == 0 else (s, 0))

    members = [(whole, corner), (even_away[0], below)]
    rows = [(corner, whole), (handed, odd)]
    states = [match([member], rows, lambda s, c: (2 * s, 2 * s + 1))[0] for member in members]
    for hop in range(1, slots // 4):
        away = swapped(pick(odd_away[hop - 1], even_away[hop - 1]))
        rows = [(odd_away[hop - 1], even_away[hop - 1]), (away, away)]

        def ids(s, c):
            source = lax.rem(s - 4 * hop + slots, slots)
            return 2 * source + 1 - c, 2 * source + c

        states = match(members, rows, ids, states)
    state, other = states
    corner_state = routed(state, lambda s, c: (s ^ (1 if c == 0 else 3), c))
    near_state = routed(other, lambda s, c: (s ^ (1 if c == 0 else 2), c))
    own = combined(pick(state, corner_state), near_state, scale)
    total = combined(own, swapped(own), scale)
    columns = jnp.arange(row_width, dtype=jnp.int32).astype(jnp.float32) * CELL
    flow_x = total[2] / total[1] - columns
    flow_y = total[3] / total[1] - slot.astype(jnp.float32) * CELL
    return jnp.stack([flow_x, flow_y]).reshape(2, 1, row_width)


def solution(mesh):
    placed = (
        P(("groups", "query"), None, None),
        P(("groups", "query", "target"), None, None),
        P(),
        P(),
    )
    return jax.shard_map(
        on_device,
        mesh=mesh,
        in_specs=placed,
        out_specs=P(None, ("groups", "query"), None),
        check_vma=False,
    )
```

```python
import functools
import math

import jax
import jax.numpy as jnp
from jax import lax
from jax.experimental import pallas as pl
from jax.experimental.pallas import tpu as pltpu
from jax.sharding import PartitionSpec as P

CELL = 0.0625
LOG2E = math.log2(math.e)
VMEM_LIMIT = 32 * 1024 * 1024
RIM_VMEM = (64 * 1024 - 10944) * 1024


def column_taps(row, stage):
    out_cols = row.shape[0] // 2
    stage[pl.ds(8, row.shape[0]), :] = row.astype(jnp.float32)
    return [
        stage[pl.ds(7 + tap, out_cols, stride=2), :].astype(jnp.bfloat16) for tap in range(3)
    ]


def tap_row_sum(row, weight_ref, tap_row, stage):
    taps = column_taps(row, stage)
    total = None
    for tap_col in range(3):
        term = jnp.dot(
            taps[tap_col], weight_ref[tap_row, tap_col], preferred_element_type=jnp.float32
        )
        total = term if total is None else total + term
    return total


def rim_kernel(query_hbm, target_hbm, weight_hbm, rim_ref, near_ref, row_ref, taps_ref, sems, stage):
    first = lax.axis_index("target") == 0
    last = query_hbm.shape[0] - 1
    taps_copy = pltpu.make_async_copy(weight_hbm.at[pl.ds(0, 1)], taps_ref, sems.at[0])
    near_copy = pltpu.make_async_copy(target_hbm.at[last], near_ref, sems.at[2])

    @pl.when(first)
    def _():
        pltpu.make_async_copy(query_hbm.at[last], row_ref, sems.at[1]).start()

    @pl.when(jnp.logical_not(first))
    def _():
        pltpu.make_async_copy(target_hbm.at[last], row_ref, sems.at[1]).start()

    taps_copy.start()
    near_copy.start()
    stage[pl.ds(0, 8), :] = jnp.zeros((8, stage.shape[1]), jnp.float32)
    pltpu.make_async_copy(query_hbm.at[last], row_ref, sems.at[1]).wait()
    taps_copy.wait()
    rim_ref[...] = tap_row_sum(row_ref[...], taps_ref, 0, stage)
    near_copy.wait()


def rim_partials(query_input, target_input, conv_weight):
    _, cols, channels = query_input.shape
    out_channels = conv_weight.shape[3]
    return pl.pallas_call(
        rim_kernel,
        out_shape=(
            jax.ShapeDtypeStruct((cols // 2, out_channels), jnp.float32),
            jax.ShapeDtypeStruct((cols, channels), target_input.dtype),
        ),
        in_specs=[pl.BlockSpec(memory_space=pltpu.HBM)] * 3,
        out_specs=(pl.BlockSpec(memory_space=pltpu.VMEM),) * 2,
        scratch_shapes=[
            pltpu.VMEM((cols, channels), jnp.bfloat16),
            pltpu.VMEM((1,) + conv_weight.shape[1:], jnp.bfloat16),
            pltpu.SemaphoreType.DMA((3,)),
            pltpu.VMEM((cols + 8, channels), jnp.float32),
        ],
        compiler_params=pltpu.CompilerParams(vmem_limit_bytes=RIM_VMEM),
        name="rim_partials",
    )(query_input, target_input, conv_weight)


def odd_kernel(row_ref, weight_ref, part_ref, odd_ref, stage):
    stage[pl.ds(0, 8), :] = jnp.zeros((8, stage.shape[1]), jnp.float32)
    rim = tap_row_sum(row_ref[...], weight_ref, 0, stage)
    odd_ref[...] = (part_ref[...] + rim).astype(odd_ref.dtype)


def odd_row(row, conv_weight, part):
    cols, channels = row.shape
    return pl.pallas_call(
        odd_kernel,
        out_shape=jax.ShapeDtypeStruct(part.shape, jnp.bfloat16),
        scratch_shapes=[pltpu.VMEM((cols + 8, channels), jnp.float32)],
        compiler_params=pltpu.CompilerParams(vmem_limit_bytes=VMEM_LIMIT),
        name="odd_row",
    )(row, conv_weight, part)


def own_kernel(query_ref, target_ref, weight_ref, bias_ref, query_out, target_out, *stages):
    for stage in stages:
        stage[pl.ds(0, 8), :] = jnp.zeros((8, stage.shape[1]), jnp.float32)
    pairs = ((target_ref, target_out), (query_ref, query_out))
    for which, (frame_ref, out_ref) in enumerate(pairs):
        total = bias_ref[...]
        for tap_row in (1, 2):
            total = total + tap_row_sum(
                frame_ref[tap_row - 1], weight_ref, tap_row, stages[2 * which + tap_row - 1]
            )
        out_ref[...] = total


def own_partials(query_input, target_input, conv_weight, conv_bias):
    _, cols, channels = query_input.shape
    out_channels = conv_weight.shape[3]
    part = jax.ShapeDtypeStruct((cols // 2, out_channels), jnp.float32)
    flops = 2 * 2 * 6 * (cols // 2) * channels * out_channels
    return pl.pallas_call(
        own_kernel,
        out_shape=(part, part),
        scratch_shapes=[pltpu.VMEM((cols + 8, channels), jnp.float32)] * 4,
        compiler_params=pltpu.CompilerParams(vmem_limit_bytes=VMEM_LIMIT),
        cost_estimate=pl.CostEstimate(flops=flops, bytes_accessed=1 << 22, transcendentals=0),
        name="own_partials",
    )(query_input, target_input, conv_weight, conv_bias.reshape(1, out_channels))


def merged(state, part, scale):
    top = jnp.maximum(state[0], part[0])
    keep = jnp.exp2((state[0] - top) * scale)
    gain = jnp.exp2((part[0] - top) * scale)
    return (top, *[old * keep + new * gain for old, new in zip(state[1:], part[1:])])


def match_kernel(members, carried, row_ids, *refs):
    core = lax.axis_index("target")
    refs = list(refs)
    query_pairs = [(refs.pop(0), refs.pop(0)) for _ in range(members)]
    target_pairs = [(refs.pop(0), refs.pop(0)) for _ in range(2)]
    state_refs = [refs.pop(0) for _ in range(members if carried else 0)]
    out_refs = [refs.pop(0) for _ in range(members)]
    lanes, channels = query_pairs[0][0].shape
    steps = target_pairs[0][0].shape[0] // 8
    scale = LOG2E / math.sqrt(channels)
    offset = lax.broadcasted_iota(jnp.int32, (8, lanes), 0).astype(jnp.float32)
    targets = [jnp.where(core == 0, one[...], two[...]) for one, two in target_pairs]
    for member, (one, two) in enumerate(query_pairs):
        queries = jnp.where(core == 0, one[...], two[...])
        for share in range(2):
            refs[2 * member + share][...] = lax.dot_general(
                targets[share],
                queries,
                (((1,), (1,)), ((), ())),
                preferred_element_type=jnp.float32,
            )
    for member, out_ref in enumerate(out_refs):
        state = None
        if carried:
            state = tuple(state_refs[member][pl.ds(i, 1), :] for i in range(4))
        for share, row_id in enumerate(row_ids(lax.axis_index("query"), core)):
            scores_ref = refs[2 * member + share]
            highest = scores_ref[pl.ds(0, 8), :]
            for step in range(1, steps):
                highest = jnp.maximum(highest, scores_ref[pl.ds(8 * step, 8), :])
            highest = jnp.max(highest, axis=0, keepdims=True)
            spread = jnp.broadcast_to(highest, (8, lanes))
            plain = jnp.zeros((8, lanes), jnp.float32)
            stacked = jnp.zeros((8, lanes), jnp.float32)
            for step in reversed(range(steps)):
                plain = plain + jnp.exp2((scores_ref[pl.ds(8 * step, 8), :] - spread) * scale)
                if step:
                    stacked = stacked + plain
            part_x = jnp.sum(8.0 * stacked + offset * plain, axis=0, keepdims=True) * CELL
            part_sum = jnp.sum(plain, axis=0, keepdims=True)
            part = (highest, part_sum, part_x, part_sum * (row_id.astype(jnp.float32) * CELL))
            state = part if state is None else merged(state, part, scale)
        out_ref[...] = jnp.concatenate(state, axis=0)


def match(members, targets, row_ids, states=()):
    lanes, channels = members[0][0].shape
    row_width = targets[0][0].shape[0]
    count = len(members)
    operands = [ref for pair in (*members, *targets) for ref in pair] + list(states)
    vmem = pl.BlockSpec(memory_space=pltpu.VMEM)
    return pl.pallas_call(
        functools.partial(match_kernel, count, bool(states), row_ids),
        out_shape=(jax.ShapeDtypeStruct((4, lanes), jnp.float32),) * count,
        in_specs=[vmem] * len(operands),
        out_specs=(vmem,) * count,
        scratch_shapes=[pltpu.VMEM((row_width, lanes), jnp.float32)] * (2 * count),
        compiler_params=pltpu.CompilerParams(vmem_limit_bytes=VMEM_LIMIT),
        cost_estimate=pl.CostEstimate(
            flops=4 * count * lanes * row_width * channels,
            bytes_accessed=1 << 22,
            transcendentals=2 * count * lanes * row_width,
        ),
        name="match",
    )(*operands)


def combined(first, second, scale):
    highest = jnp.maximum(first[..., :1, :], second[..., :1, :])
    first_scale = jnp.exp2((first[..., :1, :] - highest) * scale)
    second_scale = jnp.exp2((second[..., :1, :] - highest) * scale)
    sums = first[..., 1:, :] * first_scale + second[..., 1:, :] * second_scale
    return jnp.concatenate([highest, sums], axis=-2)


def routed(value, route):
    slots, cores = lax.axis_size("query"), lax.axis_size("target")
    pairs = []
    for slot in range(slots):
        for core in range(cores):
            to = route(slot, core)
            if to is not None:
                pairs.append((slot * cores + core, to[0] * cores + to[1]))
    return lax.ppermute(value, ("query", "target"), pairs)


def on_device(query_input, target_input, conv_weight, conv_bias):
    slot = lax.axis_index("query")
    core = lax.axis_index("target")
    slots = lax.axis_size("query")
    row_width = query_input.shape[1] // 2
    channels = conv_weight.shape[3]
    scale = LOG2E / math.sqrt(channels)
    first = core == 0

    def pick(on_first, on_second):
        return jnp.where(first, on_first, on_second)

    def swapped(value):
        return routed(value, lambda s, c: (s, 1 - c))

    far_rim, near_row = rim_partials(query_input, target_input, conv_weight)
    near_row = swapped(near_row)
    far_rim = routed(far_rim, lambda s, c: ((s + 1) % slots, c))
    far_rim = jnp.where(slot == 0, 0.0, far_rim)
    query_part, target_part = own_partials(query_input, target_input, conv_weight, conv_bias)
    odd = odd_row(near_row, conv_weight, target_part)
    handed = swapped(pick(target_part, odd.astype(jnp.float32)))
    odd_away = [
        routed(odd, lambda s, c: (s, 1) if c == 0 else ((s + 4 * hop) % slots, 0))
        for hop in range(1, max(2, slots // 4))
    ]
    whole = (pick(query_part, handed) + far_rim).astype(jnp.bfloat16)
    handed = handed.astype(jnp.bfloat16)
    even_away = [
        routed(whole, lambda s, c: (s ^ 1, 0) if c == 0 else ((s + 4 * hop) % slots, 1))
        for hop in range(1, max(2, slots // 4))
    ]
    below = routed(whole, lambda s, c: (s ^ 2, 1) if c == 0 else (s, 0))
    corner = routed(whole, lambda s, c: (s ^ 3, 1) if c == 0 else (s, 0))

    members = [(whole, corner), (even_away[0], below)]
    rows = [(corner, whole), (handed, odd)]
    states = [match([member], rows, lambda s, c: (2 * s, 2 * s + 1))[0] for member in members]
    for hop in range(1, slots // 4):
        away = swapped(pick(odd_away[hop - 1], even_away[hop - 1]))
        rows = [(odd_away[hop - 1], even_away[hop - 1]), (away, away)]

        def ids(s, c):
            source = lax.rem(s - 4 * hop + slots, slots)
            return 2 * source + 1 - c, 2 * source + c

        states = match(members, rows, ids, states)
    state, other = states
    corner_state = routed(state, lambda s, c: (s ^ (1 if c == 0 else 3), c))
    near_state = routed(other, lambda s, c: (s ^ (1 if c == 0 else 2), c))
    own = combined(pick(state, corner_state), near_state, scale)
    total = combined(own, swapped(own), scale)
    columns = jnp.arange(row_width, dtype=jnp.int32).astype(jnp.float32) * CELL
    flow_x = total[2] / total[1] - columns
    flow_y = total[3] / total[1] - slot.astype(jnp.float32) * CELL
    return jnp.stack([flow_x, flow_y]).reshape(2, 1, row_width)


def solution(mesh):
    placed = (
        P(("groups", "query"), None, None),
        P(("groups", "query", "target"), None, None),
        P(),
        P(),
    )
    return jax.shard_map(
        on_device,
        mesh=mesh,
        in_specs=placed,
        out_specs=P(None, ("groups", "query"), None),
        check_vma=False,
    )
```

```python
import functools
import math

import jax
import jax.numpy as jnp
from jax import lax
from jax.experimental import pallas as pl
from jax.experimental.pallas import tpu as pltpu
from jax.sharding import PartitionSpec as P

CELL = 0.0625
LOG2E = math.log2(math.e)
VMEM_LIMIT = 32 * 1024 * 1024
RIM_VMEM = (64 * 1024 - 10944) * 1024


def column_taps(row, stage):
    out_cols = row.shape[0] // 2
    stage[pl.ds(8, row.shape[0]), :] = row.astype(jnp.float32)
    return [
        stage[pl.ds(7 + tap, out_cols, stride=2), :].astype(jnp.bfloat16) for tap in range(3)
    ]


def tap_row_sum(row, weight_ref, tap_row, stage):
    taps = column_taps(row, stage)
    total = None
    for tap_col in range(3):
        term = jnp.dot(
            taps[tap_col], weight_ref[tap_row, tap_col], preferred_element_type=jnp.float32
        )
        total = term if total is None else total + term
    return total


def rim_kernel(query_hbm, target_hbm, weight_hbm, rim_ref, near_ref, row_ref, taps_ref, sems, stage):
    first = lax.axis_index("target") == 0
    last = query_hbm.shape[0] - 1
    taps_copy = pltpu.make_async_copy(weight_hbm.at[pl.ds(0, 1)], taps_ref, sems.at[0])
    near_copy = pltpu.make_async_copy(target_hbm.at[last], near_ref, sems.at[2])

    @pl.when(first)
    def _():
        pltpu.make_async_copy(query_hbm.at[last], row_ref, sems.at[1]).start()

    @pl.when(jnp.logical_not(first))
    def _():
        pltpu.make_async_copy(target_hbm.at[last], row_ref, sems.at[1]).start()

    taps_copy.start()
    near_copy.start()
    stage[pl.ds(0, 8), :] = jnp.zeros((8, stage.shape[1]), jnp.float32)
    pltpu.make_async_copy(query_hbm.at[last], row_ref, sems.at[1]).wait()
    taps_copy.wait()
    rim_ref[...] = tap_row_sum(row_ref[...], taps_ref, 0, stage)
    near_copy.wait()


def rim_partials(query_input, target_input, conv_weight):
    _, cols, channels = query_input.shape
    out_channels = conv_weight.shape[3]
    return pl.pallas_call(
        rim_kernel,
        out_shape=(
            jax.ShapeDtypeStruct((cols // 2, out_channels), jnp.float32),
            jax.ShapeDtypeStruct((cols, channels), target_input.dtype),
        ),
        in_specs=[pl.BlockSpec(memory_space=pltpu.HBM)] * 3,
        out_specs=(pl.BlockSpec(memory_space=pltpu.VMEM),) * 2,
        scratch_shapes=[
            pltpu.VMEM((cols, channels), jnp.bfloat16),
            pltpu.VMEM((1,) + conv_weight.shape[1:], jnp.bfloat16),
            pltpu.SemaphoreType.DMA((3,)),
            pltpu.VMEM((cols + 8, channels), jnp.float32),
        ],
        compiler_params=pltpu.CompilerParams(vmem_limit_bytes=RIM_VMEM),
        name="rim_partials",
    )(query_input, target_input, conv_weight)


def odd_kernel(row_ref, weight_ref, part_ref, odd_ref, stage):
    stage[pl.ds(0, 8), :] = jnp.zeros((8, stage.shape[1]), jnp.float32)
    rim = tap_row_sum(row_ref[...], weight_ref, 0, stage)
    odd_ref[...] = (part_ref[...] + rim).astype(odd_ref.dtype)


def odd_row(row, conv_weight, part):
    cols, channels = row.shape
    return pl.pallas_call(
        odd_kernel,
        out_shape=jax.ShapeDtypeStruct(part.shape, jnp.bfloat16),
        scratch_shapes=[pltpu.VMEM((cols + 8, channels), jnp.float32)],
        compiler_params=pltpu.CompilerParams(vmem_limit_bytes=VMEM_LIMIT),
        name="odd_row",
    )(row, conv_weight, part)


def own_kernel(query_ref, target_ref, weight_ref, bias_ref, query_out, target_out, *stages):
    for stage in stages:
        stage[pl.ds(0, 8), :] = jnp.zeros((8, stage.shape[1]), jnp.float32)
    pairs = ((target_ref, target_out), (query_ref, query_out))
    for which, (frame_ref, out_ref) in enumerate(pairs):
        total = bias_ref[...]
        for tap_row in (1, 2):
            total = total + tap_row_sum(
                frame_ref[tap_row - 1], weight_ref, tap_row, stages[2 * which + tap_row - 1]
            )
        out_ref[...] = total


def own_partials(query_input, target_input, conv_weight, conv_bias):
    _, cols, channels = query_input.shape
    out_channels = conv_weight.shape[3]
    part = jax.ShapeDtypeStruct((cols // 2, out_channels), jnp.float32)
    flops = 2 * 2 * 6 * (cols // 2) * channels * out_channels
    return pl.pallas_call(
        own_kernel,
        out_shape=(part, part),
        scratch_shapes=[pltpu.VMEM((cols + 8, channels), jnp.float32)] * 4,
        compiler_params=pltpu.CompilerParams(vmem_limit_bytes=VMEM_LIMIT),
        cost_estimate=pl.CostEstimate(flops=flops, bytes_accessed=1 << 22, transcendentals=0),
        name="own_partials",
    )(query_input, target_input, conv_weight, conv_bias.reshape(1, out_channels))


def merged(state, part, scale):
    top = jnp.maximum(state[0], part[0])
    keep = jnp.exp2((state[0] - top) * scale)
    gain = jnp.exp2((part[0] - top) * scale)
    return (top, *[old * keep + new * gain for old, new in zip(state[1:], part[1:])])


def match_kernel(members, carried, row_ids, *refs):
    core = lax.axis_index("target")
    refs = list(refs)
    query_pairs = [(refs.pop(0), refs.pop(0)) for _ in range(members)]
    target_pairs = [(refs.pop(0), refs.pop(0)) for _ in range(2)]
    state_refs = [refs.pop(0) for _ in range(members if carried else 0)]
    out_refs = [refs.pop(0) for _ in range(members)]
    lanes, channels = query_pairs[0][0].shape
    steps = target_pairs[0][0].shape[0] // 8
    scale = LOG2E / math.sqrt(channels)
    offset = lax.broadcasted_iota(jnp.int32, (8, lanes), 0).astype(jnp.float32)
    targets = [jnp.where(core == 0, one[...], two[...]) for one, two in target_pairs]
    for member, (one, two) in enumerate(query_pairs):
        queries = jnp.where(core == 0, one[...], two[...])
        for share in range(2):
            refs[2 * member + share][...] = lax.dot_general(
                targets[share],
                queries,
                (((1,), (1,)), ((), ())),
                preferred_element_type=jnp.float32,
            )
    for member, out_ref in enumerate(out_refs):
        state = None
        if carried:
            state = tuple(state_refs[member][pl.ds(i, 1), :] for i in range(4))
        for share, row_id in enumerate(row_ids(lax.axis_index("query"), core)):
            scores_ref = refs[2 * member + share]
            highest = scores_ref[pl.ds(0, 8), :]
            for step in range(1, steps):
                highest = jnp.maximum(highest, scores_ref[pl.ds(8 * step, 8), :])
            highest = jnp.max(highest, axis=0, keepdims=True)
            spread = jnp.broadcast_to(highest, (8, lanes))
            plain = jnp.zeros((8, lanes), jnp.float32)
            stacked = jnp.zeros((8, lanes), jnp.float32)
            for step in reversed(range(steps)):
                plain = plain + jnp.exp2((scores_ref[pl.ds(8 * step, 8), :] - spread) * scale)
                if step:
                    stacked = stacked + plain
            part_x = jnp.sum(8.0 * stacked + offset * plain, axis=0, keepdims=True) * CELL
            part_sum = jnp.sum(plain, axis=0, keepdims=True)
            part = (highest, part_sum, part_x, part_sum * (row_id.astype(jnp.float32) * CELL))
            state = part if state is None else merged(state, part, scale)
        out_ref[...] = jnp.concatenate(state, axis=0)


def match(members, targets, row_ids, states=()):
    lanes, channels = members[0][0].shape
    row_width = targets[0][0].shape[0]
    count = len(members)
    operands = [ref for pair in (*members, *targets) for ref in pair] + list(states)
    vmem = pl.BlockSpec(memory_space=pltpu.VMEM)
    return pl.pallas_call(
        functools.partial(match_kernel, count, bool(states), row_ids),
        out_shape=(jax.ShapeDtypeStruct((4, lanes), jnp.float32),) * count,
        in_specs=[vmem] * len(operands),
        out_specs=(vmem,) * count,
        scratch_shapes=[pltpu.VMEM((row_width, lanes), jnp.float32)] * (2 * count),
        compiler_params=pltpu.CompilerParams(vmem_limit_bytes=VMEM_LIMIT),
        cost_estimate=pl.CostEstimate(
            flops=4 * count * lanes * row_width * channels,
            bytes_accessed=1 << 22,
            transcendentals=2 * count * lanes * row_width,
        ),
        name="match",
    )(*operands)


def combined(first, second, scale):
    highest = jnp.maximum(first[..., :1, :], second[..., :1, :])
    first_scale = jnp.exp2((first[..., :1, :] - highest) * scale)
    second_scale = jnp.exp2((second[..., :1, :] - highest) * scale)
    sums = first[..., 1:, :] * first_scale + second[..., 1:, :] * second_scale
    return jnp.concatenate([highest, sums], axis=-2)


def routed(value, route):
    slots, cores = lax.axis_size("query"), lax.axis_size("target")
    pairs = []
    for slot in range(slots):
        for core in range(cores):
            to = route(slot, core)
            if to is not None:
                pairs.append((slot * cores + core, to[0] * cores + to[1]))
    return lax.ppermute(value, ("query", "target"), pairs)


def on_device(query_input, target_input, conv_weight, conv_bias):
    slot = lax.axis_index("query")
    core = lax.axis_index("target")
    slots = lax.axis_size("query")
    row_width = query_input.shape[1] // 2
    channels = conv_weight.shape[3]
    scale = LOG2E / math.sqrt(channels)
    first = core == 0

    def pick(on_first, on_second):
        return jnp.where(first, on_first, on_second)

    def swapped(value):
        return routed(value, lambda s, c: (s, 1 - c))

    far_rim, near_row = rim_partials(query_input, target_input, conv_weight)
    near_row = swapped(near_row)
    far_rim = routed(far_rim, lambda s, c: ((s + 1) % slots, c))
    far_rim = jnp.where(slot == 0, 0.0, far_rim)
    query_part, target_part = own_partials(query_input, target_input, conv_weight, conv_bias)
    odd = odd_row(near_row, conv_weight, target_part)
    handed = swapped(pick(target_part, odd.astype(jnp.float32)))
    odd_away = [
        routed(odd, lambda s, c: (s, 1) if c == 0 else ((s + 4 * hop) % slots, 0))
        for hop in range(1, max(2, slots // 4))
    ]
    whole = (pick(query_part, handed) + far_rim).astype(jnp.bfloat16)
    handed = handed.astype(jnp.bfloat16)
    even_away = [
        routed(whole, lambda s, c: (s ^ 1, 0) if c == 0 else ((s + 4 * hop) % slots, 1))
        for hop in range(1, max(2, slots // 4))
    ]
    below = routed(whole, lambda s, c: (s ^ 2, 1) if c == 0 else (s, 0))
    corner = routed(whole, lambda s, c: (s ^ 3, 1) if c == 0 else (s, 0))

    members = [(whole, corner), (even_away[0], below)]
    rows = [(below, whole), (handed, odd)]
    states = [match([member], rows, lambda s, c: (2 * s, 2 * s + 1))[0] for member in members]
    for hop in range(1, slots // 4):
        away = swapped(pick(odd_away[hop - 1], even_away[hop - 1]))
        rows = [(odd_away[hop - 1], even_away[hop - 1]), (away, away)]

        def ids(s, c):
            source = lax.rem(s - 4 * hop + slots, slots)
            return 2 * source + 1 - c, 2 * source + c

        states = match(members, rows, ids, states)
    state, other = states
    corner_state = routed(state, lambda s, c: (s ^ (1 if c == 0 else 3), c))
    near_state = routed(other, lambda s, c: (s ^ (1 if c == 0 else 2), c))
    own = combined(pick(state, corner_state), near_state, scale)
    total = combined(own, swapped(own), scale)
    columns = jnp.arange(row_width, dtype=jnp.int32).astype(jnp.float32) * CELL
    flow_x = total[2] / total[1] - columns
    flow_y = total[3] / total[1] - slot.astype(jnp.float32) * CELL
    return jnp.stack([flow_x, flow_y]).reshape(2, 1, row_width)


def solution(mesh):
    placed = (
        P(("groups", "query"), None, None),
        P(("groups", "query", "target"), None, None),
        P(),
        P(),
    )
    return jax.shard_map(
        on_device,
        mesh=mesh,
        in_specs=placed,
        out_specs=P(None, ("groups", "query"), None),
        check_vma=False,
    )
```

```python
import functools
import math

import jax
import jax.numpy as jnp
from jax import lax
from jax.experimental import pallas as pl
from jax.experimental.pallas import tpu as pltpu
from jax.sharding import PartitionSpec as P

CELL = 0.0625
LOG2E = math.log2(math.e)
VMEM_LIMIT = 32 * 1024 * 1024
RIM_VMEM = (64 * 1024 - 10944) * 1024


def column_taps(row, stage):
    out_cols = row.shape[0] // 2
    stage[pl.ds(8, row.shape[0]), :] = row.astype(jnp.float32)
    return [
        stage[pl.ds(7 + tap, out_cols, stride=2), :].astype(jnp.bfloat16) for tap in range(3)
    ]


def tap_row_sum(row, weight_ref, tap_row, stage):
    taps = column_taps(row, stage)
    total = None
    for tap_col in range(3):
        term = jnp.dot(
            taps[tap_col], weight_ref[tap_row, tap_col], preferred_element_type=jnp.float32
        )
        total = term if total is None else total + term
    return total


def rim_kernel(query_hbm, target_hbm, weight_hbm, rim_ref, near_ref, row_ref, taps_ref, sems, stage):
    first = lax.axis_index("target") == 0
    last = query_hbm.shape[0] - 1
    taps_copy = pltpu.make_async_copy(weight_hbm.at[pl.ds(0, 1)], taps_ref, sems.at[0])
    near_copy = pltpu.make_async_copy(target_hbm.at[last], near_ref, sems.at[2])

    @pl.when(first)
    def _():
        pltpu.make_async_copy(query_hbm.at[last], row_ref, sems.at[1]).start()

    @pl.when(jnp.logical_not(first))
    def _():
        pltpu.make_async_copy(target_hbm.at[last], row_ref, sems.at[1]).start()

    taps_copy.start()
    near_copy.start()
    stage[pl.ds(0, 8), :] = jnp.zeros((8, stage.shape[1]), jnp.float32)
    pltpu.make_async_copy(query_hbm.at[last], row_ref, sems.at[1]).wait()
    taps_copy.wait()
    rim_ref[...] = tap_row_sum(row_ref[...], taps_ref, 0, stage)
    near_copy.wait()


def rim_partials(query_input, target_input, conv_weight):
    _, cols, channels = query_input.shape
    out_channels = conv_weight.shape[3]
    return pl.pallas_call(
        rim_kernel,
        out_shape=(
            jax.ShapeDtypeStruct((cols // 2, out_channels), jnp.float32),
            jax.ShapeDtypeStruct((cols, channels), target_input.dtype),
        ),
        in_specs=[pl.BlockSpec(memory_space=pltpu.HBM)] * 3,
        out_specs=(pl.BlockSpec(memory_space=pltpu.VMEM),) * 2,
        scratch_shapes=[
            pltpu.VMEM((cols, channels), jnp.bfloat16),
            pltpu.VMEM((1,) + conv_weight.shape[1:], jnp.bfloat16),
            pltpu.SemaphoreType.DMA((3,)),
            pltpu.VMEM((cols + 8, channels), jnp.float32),
        ],
        compiler_params=pltpu.CompilerParams(vmem_limit_bytes=RIM_VMEM),
        name="rim_partials",
    )(query_input, target_input, conv_weight)


def odd_kernel(row_ref, weight_ref, part_ref, odd_ref, stage):
    stage[pl.ds(0, 8), :] = jnp.zeros((8, stage.shape[1]), jnp.float32)
    rim = tap_row_sum(row_ref[...], weight_ref, 0, stage)
    odd_ref[...] = (part_ref[...] + rim).astype(odd_ref.dtype)


def odd_row(row, conv_weight, part):
    cols, channels = row.shape
    return pl.pallas_call(
        odd_kernel,
        out_shape=jax.ShapeDtypeStruct(part.shape, jnp.bfloat16),
        scratch_shapes=[pltpu.VMEM((cols + 8, channels), jnp.float32)],
        compiler_params=pltpu.CompilerParams(vmem_limit_bytes=VMEM_LIMIT),
        name="odd_row",
    )(row, conv_weight, part)


def own_kernel(query_ref, target_ref, weight_ref, bias_ref, query_out, target_out, *stages):
    for stage in stages:
        stage[pl.ds(0, 8), :] = jnp.zeros((8, stage.shape[1]), jnp.float32)
    pairs = ((target_ref, target_out), (query_ref, query_out))
    for which, (frame_ref, out_ref) in enumerate(pairs):
        total = bias_ref[...]
        for tap_row in (1, 2):
            total = total + tap_row_sum(
                frame_ref[tap_row - 1], weight_ref, tap_row, stages[2 * which + tap_row - 1]
            )
        out_ref[...] = total


def own_partials(query_input, target_input, conv_weight, conv_bias):
    _, cols, channels = query_input.shape
    out_channels = conv_weight.shape[3]
    part = jax.ShapeDtypeStruct((cols // 2, out_channels), jnp.float32)
    flops = 2 * 2 * 6 * (cols // 2) * channels * out_channels
    return pl.pallas_call(
        own_kernel,
        out_shape=(part, part),
        scratch_shapes=[pltpu.VMEM((cols + 8, channels), jnp.float32)] * 4,
        compiler_params=pltpu.CompilerParams(vmem_limit_bytes=VMEM_LIMIT),
        cost_estimate=pl.CostEstimate(flops=flops, bytes_accessed=1 << 22, transcendentals=0),
        name="own_partials",
    )(query_input, target_input, conv_weight, conv_bias.reshape(1, out_channels))


def merged(state, part, scale):
    top = jnp.maximum(state[0], part[0])
    keep = jnp.exp2((state[0] - top) * scale)
    gain = jnp.exp2((part[0] - top) * scale)
    return (top, *[old * keep + new * gain for old, new in zip(state[1:], part[1:])])


def match_kernel(members, carried, row_ids, *refs):
    core = lax.axis_index("target")
    refs = list(refs)
    query_pairs = [(refs.pop(0), refs.pop(0)) for _ in range(members)]
    target_pairs = [(refs.pop(0), refs.pop(0)) for _ in range(2)]
    state_refs = [refs.pop(0) for _ in range(members if carried else 0)]
    out_refs = [refs.pop(0) for _ in range(members)]
    lanes, channels = query_pairs[0][0].shape
    steps = target_pairs[0][0].shape[0] // 8
    scale = LOG2E / math.sqrt(channels)
    offset = lax.broadcasted_iota(jnp.int32, (8, lanes), 0).astype(jnp.float32)
    targets = [jnp.where(core == 0, one[...], two[...]) for one, two in target_pairs]
    for member, (one, two) in enumerate(query_pairs):
        queries = jnp.where(core == 0, one[...], two[...])
        for share in range(2):
            refs[2 * member + share][...] = lax.dot_general(
                targets[share],
                queries,
                (((1,), (1,)), ((), ())),
                preferred_element_type=jnp.float32,
            )
    for member, out_ref in enumerate(out_refs):
        state = None
        if carried:
            state = tuple(state_refs[member][pl.ds(i, 1), :] for i in range(4))
        for share, row_id in enumerate(row_ids(lax.axis_index("query"), core)):
            scores_ref = refs[2 * member + share]
            highest = scores_ref[pl.ds(0, 8), :]
            for step in range(1, steps):
                highest = jnp.maximum(highest, scores_ref[pl.ds(8 * step, 8), :])
            highest = jnp.max(highest, axis=0, keepdims=True)
            spread = jnp.broadcast_to(highest, (8, lanes))
            plain = jnp.zeros((8, lanes), jnp.float32)
            stacked = jnp.zeros((8, lanes), jnp.float32)
            for step in reversed(range(steps)):
                plain = plain + jnp.exp2((scores_ref[pl.ds(8 * step, 8), :] - spread) * scale)
                if step:
                    stacked = stacked + plain
            part_x = jnp.sum(8.0 * stacked + offset * plain, axis=0, keepdims=True) * CELL
            part_sum = jnp.sum(plain, axis=0, keepdims=True)
            part = (highest, part_sum, part_x, part_sum * (row_id.astype(jnp.float32) * CELL))
            state = part if state is None else merged(state, part, scale)
        out_ref[...] = jnp.concatenate(state, axis=0)


def match(members, targets, row_ids, states=()):
    lanes, channels = members[0][0].shape
    row_width = targets[0][0].shape[0]
    count = len(members)
    operands = [ref for pair in (*members, *targets) for ref in pair] + list(states)
    vmem = pl.BlockSpec(memory_space=pltpu.VMEM)
    return pl.pallas_call(
        functools.partial(match_kernel, count, bool(states), row_ids),
        out_shape=(jax.ShapeDtypeStruct((4, lanes), jnp.float32),) * count,
        in_specs=[vmem] * len(operands),
        out_specs=(vmem,) * count,
        scratch_shapes=[pltpu.VMEM((row_width, lanes), jnp.float32)] * (2 * count),
        compiler_params=pltpu.CompilerParams(vmem_limit_bytes=VMEM_LIMIT),
        cost_estimate=pl.CostEstimate(
            flops=4 * count * lanes * row_width * channels,
            bytes_accessed=1 << 22,
            transcendentals=2 * count * lanes * row_width,
        ),
        name="match",
    )(*operands)


def combined(first, second, scale):
    highest = jnp.maximum(first[..., :1, :], second[..., :1, :])
    first_scale = jnp.exp2((first[..., :1, :] - highest) * scale)
    second_scale = jnp.exp2((second[..., :1, :] - highest) * scale)
    sums = first[..., 1:, :] * first_scale + second[..., 1:, :] * second_scale
    return jnp.concatenate([highest, sums], axis=-2)


def finish_kernel(scale, own_ref, other_ref, flow_ref):
    slot = lax.axis_index("query")
    state = merged(
        tuple(own_ref[pl.ds(i, 1), :] for i in range(4)),
        tuple(other_ref[pl.ds(i, 1), :] for i in range(4)),
        scale,
    )
    columns = lax.broadcasted_iota(jnp.int32, state[0].shape, 1).astype(jnp.float32) * CELL
    flow_ref[0] = state[2] / state[1] - columns
    flow_ref[1] = state[3] / state[1] - slot.astype(jnp.float32) * CELL


def finished(own, other, scale):
    lanes = own.shape[1]
    vmem = pl.BlockSpec(memory_space=pltpu.VMEM)
    return pl.pallas_call(
        functools.partial(finish_kernel, scale),
        out_shape=jax.ShapeDtypeStruct((2, 1, lanes), jnp.float32),
        in_specs=[vmem, vmem],
        out_specs=vmem,
        compiler_params=pltpu.CompilerParams(vmem_limit_bytes=VMEM_LIMIT),
        name="finish",
    )(own, other)


def routed(value, route):
    slots, cores = lax.axis_size("query"), lax.axis_size("target")
    pairs = []
    for slot in range(slots):
        for core in range(cores):
            to = route(slot, core)
            if to is not None:
                pairs.append((slot * cores + core, to[0] * cores + to[1]))
    return lax.ppermute(value, ("query", "target"), pairs)


def on_device(query_input, target_input, conv_weight, conv_bias):
    slot = lax.axis_index("query")
    core = lax.axis_index("target")
    slots = lax.axis_size("query")
    channels = conv_weight.shape[3]
    scale = LOG2E / math.sqrt(channels)
    first = core == 0

    def pick(on_first, on_second):
        return jnp.where(first, on_first, on_second)

    def swapped(value):
        return routed(value, lambda s, c: (s, 1 - c))

    far_rim, near_row = rim_partials(query_input, target_input, conv_weight)
    near_row = swapped(near_row)
    far_rim = routed(far_rim, lambda s, c: ((s + 1) % slots, c))
    far_rim = jnp.where(slot == 0, 0.0, far_rim)
    query_part, target_part = own_partials(query_input, target_input, conv_weight, conv_bias)
    odd = odd_row(near_row, conv_weight, target_part)
    handed = swapped(pick(target_part, odd.astype(jnp.float32)))
    odd_away = [
        routed(odd, lambda s, c: (s, 1) if c == 0 else ((s + 4 * hop) % slots, 0))
        for hop in range(1, max(2, slots // 4))
    ]
    whole = (pick(query_part, handed) + far_rim).astype(jnp.bfloat16)
    handed = handed.astype(jnp.bfloat16)
    even_away = [
        routed(whole, lambda s, c: (s ^ 1, 0) if c == 0 else ((s + 4 * hop) % slots, 1))
        for hop in range(1, max(2, slots // 4))
    ]
    below = routed(whole, lambda s, c: (s ^ 2, 1) if c == 0 else (s, 0))
    corner = routed(whole, lambda s, c: (s ^ 3, 1) if c == 0 else (s, 0))

    members = [(whole, corner), (even_away[0], below)]
    rows = [(below, whole), (handed, odd)]
    states = [match([member], rows, lambda s, c: (2 * s, 2 * s + 1))[0] for member in members]
    for hop in range(1, slots // 4):
        away = swapped(pick(odd_away[hop - 1], even_away[hop - 1]))
        rows = [(odd_away[hop - 1], even_away[hop - 1]), (away, away)]

        def ids(s, c):
            source = lax.rem(s - 4 * hop + slots, slots)
            return 2 * source + 1 - c, 2 * source + c

        states = match(members, rows, ids, states)
    state, other = states
    corner_state = routed(state, lambda s, c: (s ^ (1 if c == 0 else 3), c))
    near_state = routed(other, lambda s, c: (s ^ (1 if c == 0 else 2), c))
    own = combined(pick(state, corner_state), near_state, scale)
    return finished(own, swapped(own), scale)


def solution(mesh):
    placed = (
        P(("groups", "query"), None, None),
        P(("groups", "query", "target"), None, None),
        P(),
        P(),
    )
    return jax.shard_map(
        on_device,
        mesh=mesh,
        in_specs=placed,
        out_specs=P(None, ("groups", "query"), None),
        check_vma=False,
    )
```
